32 devices in a mesh: groups: 2 (over y), qring: 4 (over x, core), kvring: 4 (over z), head: 1.
Axes of the slice: x: 2, y: 2, z: 4, core: 2. Of those that a mesh axis runs over, the one named last changes fastest.
Arguments:
- queries: bfloat16 [1536, 4096], P(('groups', 'qring', 'kvring'), 'head'), parts along dimension 0, may hold values from -6 to 6
- keys: bfloat16 [1536, 512], P(('groups', 'qring', 'kvring'), 'head'), parts along dimension 0, may hold values from -6 to 6
- values: bfloat16 [1536, 512], P(('groups', 'qring', 'kvring'), 'head'), parts along dimension 0, may hold values from -6 to 6
- doc_ids: int32 [1536], P('groups'), parts along dimension 0, may hold values from 0 to 15, never falling along the last dimension, each value on 1 to 480 neighbouring positions
- head_mask: int32 [32], P('head'), may hold values 0 or 1
- w_out: bfloat16 [4096, 8192], P('head', 'kvring'), may hold values from -0.5 to 0.5
Outputs:
- mixed: bfloat16 [1536, 8192], P(('groups', 'qring', 'head'), 'kvring'), parts along dimension 0
The draws below stay inside these ranges and needn't reach their ends.
There are 2 independent parts, one for each index of `groups`. The reference program is written for one: setup_inputs(seed, part) draws one part's arguments, and reference() takes and returns one part's arrays. A program takes and returns all parts, laid end to end along the dimension named above; an argument that names none is the same for every part. Nothing has to cross between parts.
All inputs are finite; a program needn't handle non-finite values. No bound on the sum of `head_mask` on one device may be relied on, other than what follows from the above.
Results may differ from the reference program's by a relative error of at most 0.015.
Values may be sent and summed in bfloat16 or wider, within the bound.
No kernel may reach another device: no remote copies, remote signals or barrier semaphores. Data moves between devices by JAX's collectives and lax.ppermute only.
A program may use at most 64 MiB of HBM per device.

```python
import math
import jax
import jax.numpy as jnp
import numpy as np
from jax import lax

D = 8192
HEADS = 32
KVH = 4
HD = 128
GROUP = 8
DOCS = 16
SEQ = 768
LONGEST = 480


def draw_queries(key, part):
    base = jnp.clip(1.5 * jax.random.normal(jax.random.fold_in(key, 2), (SEQ, KVH, GROUP, HD), jnp.float32), -6.0, 6.0)
    return base.reshape(SEQ, HEADS * HD).astype(jnp.bfloat16)


def draw_keys(key, part):
    base = jnp.clip(jax.random.normal(jax.random.fold_in(key, 1), (SEQ, KVH, HD), jnp.float32), -6.0, 6.0)
    return base.reshape(SEQ, KVH * HD).astype(jnp.bfloat16)


def plant(drawn, stream_key, low, top_value):
    place = [jax.random.randint(jax.random.fold_in(stream_key, axis), (), 0, length) for axis, length in enumerate(drawn.shape)]
    main_axis = drawn.shape.index(max(drawn.shape))
    next_to = place[:main_axis] + [(place[main_axis] + 1) % drawn.shape[main_axis]] + place[main_axis + 1:]
    return drawn.at[tuple(place)].set(low).at[tuple(next_to)].set(top_value)


def steps_of(rng, extent, pieces, least, high):
    loudness = 1.0
    for axis_at, parts in pieces:
        draws = jax.random.uniform(jax.random.fold_in(jax.random.fold_in(rng, 6), axis_at), (parts,), jnp.float32, least / len(pieces), high / len(pieces))
        loudness = loudness * jnp.repeat(jnp.exp(draws), extent[axis_at] // parts).reshape((-1,) + (1,) * (len(extent) - 1 - axis_at))
    return loudness


def profile(amount, total, most, lean):
    portions = [(1 << 20) // math.isqrt(grade ** lean) + 1 for grade in range(2, amount + 1)]
    spare, holding = total - most - (amount - 1), [1] * (amount - 1)
    while spare > 0:
        free = [i for i in range(amount - 1) if holding[i] < most]
        pool, remaining = sum([portions[i] for i in free]), spare
        for i in free:
            more = min(most - holding[i], max(1, remaining * portions[i] // pool), spare)
            holding[i] = holding[i] + more
            spare = spare - more
    return np.array([most] + holding)


def uneven(key, count, total, most, slope):
    if count == 2:
        one = jax.random.randint(key, (), max(1, total - most), min(most, total - 1) + 1)
        return jnp.stack([one, total - one])
    lengths = jnp.asarray(profile(count, total, most, slope), jnp.int32)
    twos = (count - 1) // 2
    giver, receiver = lengths[1:1 + 2 * twos:2], lengths[2:2 + 2 * twos:2]
    slack = jnp.minimum(giver - 1, most - receiver)
    passed = jax.random.randint(jax.random.fold_in(key, 1), (twos,), 0, 1 << 20) % (slack + 1)
    lengths = lengths.at[1:1 + 2 * twos:2].set(giver - passed).at[2:2 + 2 * twos:2].set(receiver + passed)
    return lengths[jax.random.permutation(jax.random.fold_in(key, 2), count)]


def scatter_about(stream_key, extent, scale, bound, split=(), held_as=jnp.bfloat16):
    array = jax.random.normal(stream_key, extent, jnp.float32) * scale
    if len(split) > 0:
        array = steps_of(stream_key, extent, split, -0.22, 0.18) * array
    return jnp.clip(array, min=-bound, max=bound).astype(held_as)


def setup_inputs(seed: int = 0, part: int = 0) -> dict:
    splits = jax.random.split(jax.random.key(seed), 7)
    part_splits = jax.random.split(jax.random.fold_in(splits[6], part), 7)
    queries = draw_queries(jax.random.fold_in(jax.random.fold_in(splits[6], part), 71), part)
    keys = draw_keys(jax.random.fold_in(jax.random.fold_in(splits[6], part), 71), part)
    values = scatter_about(part_splits[2], (SEQ, KVH * HD), 1.0, 6.0, ((0, 16),))
    doc_ids = jnp.searchsorted(jnp.cumsum(uneven(part_splits[3], DOCS, SEQ, LONGEST, 2)), jnp.arange(SEQ), side="right").astype(jnp.int32)
    head_mask = plant((jax.random.randint(splits[4], (HEADS,), 0, 4) < 3).astype(jnp.int32), jax.random.fold_in(splits[4], 1), 0, 1)
    w_out = scatter_about(splits[5], (HEADS * HD, D), HD ** -0.5, 0.5, ((1, 4),))
    return {"queries": queries, "keys": keys, "values": values, "doc_ids": doc_ids, "head_mask": head_mask, "w_out": w_out}


NEG = -1e+30

def reference(queries, keys, values, doc_ids, head_mask, w_out):
    block_size = math.gcd(SEQ, 256)
    query_all = queries.reshape(SEQ, KVH, GROUP, HD)
    key_all = keys.reshape(SEQ, KVH, HD).astype(jnp.float32)
    value_all = values.reshape(SEQ, KVH, HD).astype(jnp.float32)
    key_pos = jnp.arange(SEQ, dtype=jnp.int32)
    mask_f = head_mask.reshape(KVH, GROUP).astype(jnp.float32)
    scale_factor = 1.0 / math.sqrt(HD)

    def one_block(index):
        start = (index * block_size).astype(jnp.int32)
        query_rows = lax.dynamic_slice_in_dim(query_all, start, block_size, 0).astype(jnp.float32)
        query_doc = lax.dynamic_slice_in_dim(doc_ids, start, block_size, 0)
        query_pos = start + jnp.arange(block_size, dtype=jnp.int32)
        visible = (query_doc[:, None] == doc_ids[None, :]) & (key_pos[None, :] <= query_pos[:, None])
        mask4 = visible[:, None, None, :]
        scores = jnp.einsum('rgec,kgc->rgek', query_rows, key_all) * scale_factor
        scores = jnp.where(mask4, scores, NEG)
        top = lax.optimization_barrier(jnp.max(scores, axis=-1))
        weights = jnp.where(mask4, jnp.exp(scores - top[..., None]), 0.0)
        total = lax.optimization_barrier(jnp.sum(weights, axis=-1))
        rounded = weights.astype(jnp.bfloat16).astype(jnp.float32)
        context = jnp.einsum('rgek,kgc->rgec', rounded, value_all)
        attended = context / total[..., None] * mask_f[None, :, :, None]
        return attended.astype(jnp.bfloat16).reshape(block_size, HEADS * HD)
    blocks = lax.map(one_block, jnp.arange(SEQ // block_size, dtype=jnp.int32))
    attended = blocks.reshape(SEQ, HEADS * HD)
    return jnp.dot(attended, w_out, preferred_element_type=jnp.float32).astype(jnp.bfloat16)
```

```python
import functools
import math

import jax
import jax.numpy as jnp
from jax import lax
from jax.experimental import pallas as pl
from jax.experimental.pallas import tpu as pltpu
from jax.sharding import PartitionSpec as P

HD = 128


NEG = -1e30


def block_rows(total_rows, shard_rows):
    best_size = shard_rows
    for multiple in range(1, total_rows // shard_rows + 1):
        if total_rows // shard_rows % multiple == 0 and multiple * shard_rows <= 256:
            best_size = multiple * shard_rows
    return best_size


def attend_keys(state, visible, queries4, key_rows, value_rows, scale_factor):
    run_max, run_sum, run_out = state
    mask4 = visible[:, None, None, :]
    scores = (
        jnp.einsum("rgec,kgc->rgek", queries4, key_rows, preferred_element_type=jnp.float32)
        * scale_factor
    )
    scores = jnp.where(mask4, scores, NEG)
    new_max = jnp.maximum(run_max, jnp.max(scores, axis=-1))
    weights = jnp.where(mask4, jnp.exp(scores - new_max[..., None]), 0.0)
    shrink = jnp.exp(run_max - new_max)
    run_sum = run_sum * shrink + jnp.sum(weights, axis=-1)
    update = jnp.einsum(
        "rgek,kgc->rgec",
        weights.astype(jnp.bfloat16),
        value_rows,
        preferred_element_type=jnp.float32,
    )
    run_out = run_out * shrink[..., None] + update
    return (new_max, run_sum, run_out)


def fold_piece(
    state, pieces, key_start, queries4, query_doc, query_pos, doc_ids, shard_rows, scale_factor
):
    key_all, value_all = pieces
    total_rows = key_all.shape[0]
    block_size = block_rows(total_rows, shard_rows)

    def one_block(index, carry):
        offset = index * block_size
        key_rows = lax.dynamic_slice_in_dim(key_all, offset, block_size, 0)
        value_rows = lax.dynamic_slice_in_dim(value_all, offset, block_size, 0)
        first = key_start + offset
        key_doc = lax.dynamic_slice_in_dim(doc_ids, first, block_size, 0)
        key_pos = first + jnp.arange(block_size, dtype=jnp.int32)
        visible = (query_doc[:, None] == key_doc[None, :]) & (
            key_pos[None, :] <= query_pos[:, None]
        )
        return attend_keys(carry, visible, queries4, key_rows, value_rows, scale_factor)

    return lax.fori_loop(0, total_rows // block_size, one_block, state)


def per_device_any_ring(queries, keys, values, doc_ids, head_mask, w_out):
    shard_rows = queries.shape[0]
    kv_local = keys.shape[1] // HD
    q_local = queries.shape[1] // HD
    per_group = q_local // kv_local
    scale_factor = 1.0 / math.sqrt(HD)
    cycle_size = lax.axis_size("kvring")
    cycle_index = lax.axis_index("kvring")
    loop_index = lax.axis_index("qring")
    quarter = cycle_size * shard_rows
    key_rows = keys.reshape(shard_rows, kv_local, HD)
    value_rows = values.reshape(shard_rows, kv_local, HD)
    loop_size = lax.axis_size("qring")
    gathered = lax.all_gather(queries, "qring", axis=0, tiled=True)
    query_total = loop_size * shard_rows
    row_ids = jnp.arange(query_total, dtype=jnp.int32)
    query_pos = row_ids // shard_rows * quarter + cycle_index * shard_rows + row_ids % shard_rows
    queries4 = gathered.reshape(query_total, kv_local, per_group, HD)
    query_doc = jnp.take(doc_ids, query_pos)
    key_base = loop_index * quarter
    initial = (
        jnp.full((query_total, kv_local, per_group), NEG, jnp.float32),
        jnp.zeros((query_total, kv_local, per_group), jnp.float32),
        jnp.zeros((query_total, kv_local, per_group, HD), jnp.float32),
    )
    run_max, run_sum, run_out = fold_piece(
        initial,
        (
            lax.all_gather(key_rows, "kvring", axis=0, tiled=True),
            lax.all_gather(value_rows, "kvring", axis=0, tiled=True),
        ),
        key_base,
        queries4,
        query_doc,
        query_pos,
        doc_ids,
        shard_rows,
        scale_factor,
    )
    top = lax.pmax(run_max, "qring")
    factor = jnp.exp(run_max - top)
    numer, denom = (
        lax.psum_scatter(
            (run_out * factor[..., None]).astype(jnp.bfloat16),
            "qring",
            scatter_dimension=0,
            tiled=True,
        ).astype(jnp.float32),
        lax.psum_scatter(
            (run_sum * factor).astype(jnp.bfloat16), "qring", scatter_dimension=0, tiled=True
        ).astype(jnp.float32),
    )
    mask_f = head_mask.reshape(kv_local, per_group).astype(jnp.float32)
    attended = (
        (numer / denom[..., None] * mask_f[None, :, :, None])
        .astype(jnp.bfloat16)
        .reshape(shard_rows, q_local * HD)
    )
    partial_sum = jnp.dot(
        lax.all_gather(attended, "kvring", axis=0, tiled=True),
        w_out,
        preferred_element_type=jnp.float32,
    )
    return lax.psum_scatter(
        partial_sum.astype(jnp.bfloat16), "head", scatter_dimension=0, tiled=True
    )


VMEM_LIMIT = 56 * 1024 * 1024
LOG2E = math.log2(math.e)


def small_ring(mesh):
    return (mesh.shape["qring"], mesh.shape["kvring"], mesh.shape["head"]) == (4, 4, 1)


def swap_along(array, axis_name, partner):
    size = lax.axis_size(axis_name)
    return lax.ppermute(array, axis_name, [(i, i ^ partner) for i in range(size)])


def after(array, *others):
    return lax.optimization_barrier((array, *others))[0]


def slot_of(index, width, count):
    slot = jnp.zeros_like(index)
    for bound in range(1, count):
        slot = slot + (index >= bound * width).astype(jnp.int32)
    return slot


def prep_kernel(rows, nq, nz, slots_a, slots_b, mask_ref, doc_ref, q_ref, qa_ref, qb_ref, bias_ref):
    for slot in range(slots_a + slots_b):
        block = q_ref[:, slot * HD : (slot + 1) * HD]
        if slot < slots_a:
            qa_ref[:, slot * HD : (slot + 1) * HD] = block
        else:
            qb_ref[:, (slot - slots_a) * HD : (slot - slots_a + 1) * HD] = block
    quarter = rows * nz
    total = quarter * nq
    q_at = lax.axis_index("qring")
    z_at = lax.axis_index("kvring")
    doc = doc_ref[...]
    row = lax.broadcasted_iota(jnp.int32, (quarter, 1), 0)
    row_z = slot_of(row, rows, nz)
    row_pos = q_at * quarter + (row_z ^ z_at) * rows + row - row_z * rows
    col = lax.broadcasted_iota(jnp.int32, (1, total), 1)
    col_q = slot_of(col, quarter, nq)
    rest = col - col_q * quarter
    col_z = slot_of(rest, rows, nz)
    col_pos = (col_q ^ q_at) * quarter + (col_z ^ z_at) * rows + rest - col_z * rows
    own_doc = jnp.sum(jnp.where(col == row_pos, doc, 0), axis=1, keepdims=True)
    first = jnp.sum((doc < own_doc).astype(jnp.int32), axis=1, keepdims=True)
    bias_ref[...] = jnp.where((col_pos >= first) & (col_pos <= row_pos), 0.0, NEG)


def attend_slots(nz, slots, first_slot, kv_refs, q_refs, bias_ref, mask_ref, att_ref):
    heads = mask_ref.shape[0]
    kv_heads = kv_refs[0].shape[1] // (2 * HD)
    scale = LOG2E / math.sqrt(HD)

    def one_slot(slot):
        head = first_slot + slot
        at = pl.multiple_of(slot * HD, HD)
        group = head // (heads // kv_heads)
        k_at = pl.multiple_of(group * HD, HD)
        v_at = pl.multiple_of((group + kv_heads) * HD, HD)
        q = jnp.concatenate([ref[:, pl.ds(at, HD)] for ref in q_refs], axis=0)
        k = jnp.concatenate([ref[:, pl.ds(k_at, HD)] for ref in kv_refs], axis=0)
        v = jnp.concatenate([ref[:, pl.ds(v_at, HD)] for ref in kv_refs], axis=0)
        scores = lax.dot_general(q, k, (((1,), (1,)), ((), ())), preferred_element_type=jnp.float32)
        scores = scores * scale + bias_ref[...]
        top = jnp.max(scores, axis=1, keepdims=True)
        weights = jnp.exp2(scores - top)
        total = jnp.sum(weights, axis=1, keepdims=True)
        context = jnp.dot(weights.astype(jnp.bfloat16), v, preferred_element_type=jnp.float32)
        keep = mask_ref[head].astype(jnp.float32)
        att_ref[:, pl.ds(at, HD)] = (context * (keep / total)).astype(jnp.bfloat16)

    pl.loop(0, slots, unroll=UNROLL)(one_slot)


UNROLL = 2


def w_copies(slots, first_slot, w_hbm, w_ref, sem):
    return [
        pltpu.make_async_copy(
            w_hbm.at[pl.ds((first_slot + slot) * HD, HD)],
            w_ref.at[pl.ds(slot * HD, HD)],
            sem.at[slot],
        )
        for slot in range(slots)
    ]


def first_kernel(nq, nz, slots, mask_ref, *refs):
    kv_refs, q_refs, (bias_ref, w_hbm, acc_ref, att_ref, w_ref, sem) = refs[:nq], refs[nq : nq + nz], refs[nq + nz :]
    copies = w_copies(slots, 0, w_hbm, w_ref, sem)
    for copy in copies:
        copy.start()
    attend_slots(nz, slots, 0, kv_refs, q_refs, bias_ref, mask_ref, att_ref)
    for copy in copies:
        copy.wait()
    width = 512

    def one_tile(tile):
        at = pl.ds(pl.multiple_of(tile * width, width), width)
        acc_ref[:, at] = jnp.dot(att_ref[...], w_ref[:, at], preferred_element_type=jnp.float32)

    pl.loop(0, acc_ref.shape[1] // width)(one_tile)


def last_kernel(nq, nz, first_slot, slots, mask_ref, *refs):
    kv_refs, q_refs, (bias_ref, w_hbm, acc_ref, out_ref, att_ref, w_ref, sem) = refs[:nq], refs[nq : nq + nz], refs[nq + nz :]
    copies = w_copies(slots, first_slot, w_hbm, w_ref, sem)
    for copy in copies:
        copy.start()
    attend_slots(nz, slots, first_slot, kv_refs, q_refs, bias_ref, mask_ref, att_ref)
    for copy in copies:
        copy.wait()
    width = 512
    rows = q_refs[0].shape[0]
    z_at = lax.axis_index("kvring")

    def one_tile(tile):
        at = pl.ds(pl.multiple_of(tile * width, width), width)
        mixed = acc_ref[:, at] + jnp.dot(att_ref[...], w_ref[:, at], preferred_element_type=jnp.float32)
        mixed = mixed.astype(jnp.bfloat16)
        for slot in range(nz):
            place = pl.multiple_of((z_at ^ slot) * rows, rows)
            out_ref[pl.ds(place, rows), at] = mixed[slot * rows : (slot + 1) * rows]

    pl.loop(0, acc_ref.shape[1] // width)(one_tile)


def per_device_small_ring(queries, keys, values, doc_ids, head_mask, w_out):
    rows = queries.shape[0]
    nq = lax.axis_size("qring")
    nz = lax.axis_size("kvring")
    heads = head_mask.shape[0]
    width = w_out.shape[1]
    quarter = rows * nz
    total = quarter * nq
    slots_b = heads // 4
    slots_a = heads - slots_b
    smem = pl.BlockSpec(memory_space=pltpu.SMEM)
    vmem = pl.BlockSpec(memory_space=pltpu.VMEM)
    hbm = pl.BlockSpec(memory_space=pl.ANY)

    kv_own = jnp.concatenate([keys, values], axis=1)
    kv_parts = [kv_own] + [swap_along(kv_own, "kvring", m) for m in range(1, nz)]
    qa, qb, bias = pl.pallas_call(
        functools.partial(prep_kernel, rows, nq, nz, slots_a, slots_b),
        out_shape=(
            jax.ShapeDtypeStruct((rows, slots_a * HD), jnp.bfloat16),
            jax.ShapeDtypeStruct((rows, slots_b * HD), jnp.bfloat16),
            jax.ShapeDtypeStruct((quarter, total), jnp.float32),
        ),
        in_specs=[smem, vmem, vmem],
        out_specs=(vmem, vmem, vmem),
        name="prep",
    )(head_mask, doc_ids.reshape(1, total), queries)
    kv0 = jnp.concatenate(kv_parts, axis=0)
    kv2 = swap_along(kv0, "qring", 2)
    kv1 = swap_along(kv0, "qring", 1)
    kv3 = swap_along(kv2, "qring", 1)
    kv = (kv0, kv1, kv2, kv3)
    qa = after(qa, kv_parts[1])
    qa_parts = [qa] + [swap_along(qa, "kvring", m) for m in range(1, nz)]
    qb_parts = [qb] + [swap_along(after(qb, qa_parts[m]), "kvring", m) for m in range(1, nz)]

    params = pltpu.CompilerParams(vmem_limit_bytes=VMEM_LIMIT)
    acc = pl.pallas_call(
        functools.partial(first_kernel, nq, nz, slots_a),
        out_shape=jax.ShapeDtypeStruct((quarter, width), jnp.float32),
        in_specs=[smem] + [vmem] * (nq + nz + 1) + [hbm],
        out_specs=vmem,
        scratch_shapes=[
            pltpu.VMEM((quarter, slots_a * HD), jnp.bfloat16),
            pltpu.VMEM((slots_a * HD, width), jnp.bfloat16),
            pltpu.SemaphoreType.DMA((slots_a,)),
        ],
        compiler_params=params,
        name="first",
    )(head_mask, *kv, *qa_parts, bias, w_out)
    return pl.pallas_call(
        functools.partial(last_kernel, nq, nz, slots_a, slots_b),
        out_shape=jax.ShapeDtypeStruct((quarter, width), jnp.bfloat16),
        in_specs=[smem] + [vmem] * (nq + nz + 1) + [hbm, vmem],
        out_specs=vmem,
        scratch_shapes=[
            pltpu.VMEM((quarter, slots_b * HD), jnp.bfloat16),
            pltpu.VMEM((slots_b * HD, width), jnp.bfloat16),
            pltpu.SemaphoreType.DMA((slots_b,)),
        ],
        compiler_params=params,
        name="last",
    )(head_mask, *kv, *qb_parts, bias, w_out, acc)


def solution(mesh):
    placed = (
        P(("groups", "qring", "kvring"), "head"),
        P(("groups", "qring", "kvring"), "head"),
        P(("groups", "qring", "kvring"), "head"),
        P("groups"),
        P("head"),
        P("head", "kvring"),
    )
    per_device = per_device_small_ring if small_ring(mesh) else per_device_any_ring
    return jax.shard_map(
        per_device,
        mesh=mesh,
        in_specs=placed,
        out_specs=P(("groups", "qring", "head"), "kvring"),
        check_vma=False,
    )
```

```python
import functools
import math

import jax
import jax.numpy as jnp
from jax import lax
from jax.experimental import pallas as pl
from jax.experimental.pallas import tpu as pltpu
from jax.sharding import PartitionSpec as P

HD = 128


NEG = -1e30


def block_rows(total_rows, shard_rows):
    best_size = shard_rows
    for multiple in range(1, total_rows // shard_rows + 1):
        if total_rows // shard_rows % multiple == 0 and multiple * shard_rows <= 256:
            best_size = multiple * shard_rows
    return best_size


def attend_keys(state, visible, queries4, key_rows, value_rows, scale_factor):
    run_max, run_sum, run_out = state
    mask4 = visible[:, None, None, :]
    scores = (
        jnp.einsum("rgec,kgc->rgek", queries4, key_rows, preferred_element_type=jnp.float32)
        * scale_factor
    )
    scores = jnp.where(mask4, scores, NEG)
    new_max = jnp.maximum(run_max, jnp.max(scores, axis=-1))
    weights = jnp.where(mask4, jnp.exp(scores - new_max[..., None]), 0.0)
    shrink = jnp.exp(run_max - new_max)
    run_sum = run_sum * shrink + jnp.sum(weights, axis=-1)
    update = jnp.einsum(
        "rgek,kgc->rgec",
        weights.astype(jnp.bfloat16),
        value_rows,
        preferred_element_type=jnp.float32,
    )
    run_out = run_out * shrink[..., None] + update
    return (new_max, run_sum, run_out)


def fold_piece(
    state, pieces, key_start, queries4, query_doc, query_pos, doc_ids, shard_rows, scale_factor
):
    key_all, value_all = pieces
    total_rows = key_all.shape[0]
    block_size = block_rows(total_rows, shard_rows)

    def one_block(index, carry):
        offset = index * block_size
        key_rows = lax.dynamic_slice_in_dim(key_all, offset, block_size, 0)
        value_rows = lax.dynamic_slice_in_dim(value_all, offset, block_size, 0)
        first = key_start + offset
        key_doc = lax.dynamic_slice_in_dim(doc_ids, first, block_size, 0)
        key_pos = first + jnp.arange(block_size, dtype=jnp.int32)
        visible = (query_doc[:, None] == key_doc[None, :]) & (
            key_pos[None, :] <= query_pos[:, None]
        )
        return attend_keys(carry, visible, queries4, key_rows, value_rows, scale_factor)

    return lax.fori_loop(0, total_rows // block_size, one_block, state)


def per_device_any_ring(queries, keys, values, doc_ids, head_mask, w_out):
    shard_rows = queries.shape[0]
    kv_local = keys.shape[1] // HD
    q_local = queries.shape[1] // HD
    per_group = q_local // kv_local
    scale_factor = 1.0 / math.sqrt(HD)
    cycle_size = lax.axis_size("kvring")
    cycle_index = lax.axis_index("kvring")
    loop_index = lax.axis_index("qring")
    quarter = cycle_size * shard_rows
    key_rows = keys.reshape(shard_rows, kv_local, HD)
    value_rows = values.reshape(shard_rows, kv_local, HD)
    loop_size = lax.axis_size("qring")
    gathered = lax.all_gather(queries, "qring", axis=0, tiled=True)
    query_total = loop_size * shard_rows
    row_ids = jnp.arange(query_total, dtype=jnp.int32)
    query_pos = row_ids // shard_rows * quarter + cycle_index * shard_rows + row_ids % shard_rows
    queries4 = gathered.reshape(query_total, kv_local, per_group, HD)
    query_doc = jnp.take(doc_ids, query_pos)
    key_base = loop_index * quarter
    initial = (
        jnp.full((query_total, kv_local, per_group), NEG, jnp.float32),
        jnp.zeros((query_total, kv_local, per_group), jnp.float32),
        jnp.zeros((query_total, kv_local, per_group, HD), jnp.float32),
    )
    run_max, run_sum, run_out = fold_piece(
        initial,
        (
            lax.all_gather(key_rows, "kvring", axis=0, tiled=True),
            lax.all_gather(value_rows, "kvring", axis=0, tiled=True),
        ),
        key_base,
        queries4,
        query_doc,
        query_pos,
        doc_ids,
        shard_rows,
        scale_factor,
    )
    top = lax.pmax(run_max, "qring")
    factor = jnp.exp(run_max - top)
    numer, denom = (
        lax.psum_scatter(
            (run_out * factor[..., None]).astype(jnp.bfloat16),
            "qring",
            scatter_dimension=0,
            tiled=True,
        ).astype(jnp.float32),
        lax.psum_scatter(
            (run_sum * factor).astype(jnp.bfloat16), "qring", scatter_dimension=0, tiled=True
        ).astype(jnp.float32),
    )
    mask_f = head_mask.reshape(kv_local, per_group).astype(jnp.float32)
    attended = (
        (numer / denom[..., None] * mask_f[None, :, :, None])
        .astype(jnp.bfloat16)
        .reshape(shard_rows, q_local * HD)
    )
    partial_sum = jnp.dot(
        lax.all_gather(attended, "kvring", axis=0, tiled=True),
        w_out,
        preferred_element_type=jnp.float32,
    )
    return lax.psum_scatter(
        partial_sum.astype(jnp.bfloat16), "head", scatter_dimension=0, tiled=True
    )


VMEM_LIMIT = 32 * 1024 * 1024
LOG2E = math.log2(math.e)
PAIR = 2
NEAR_SPLIT = (8, 6)
NEAR_SLOTS = sum(NEAR_SPLIT)
FAR_SLOTS = 12
TILE = 1024


def small_ring(mesh):
    return (mesh.shape["qring"], mesh.shape["kvring"], mesh.shape["head"]) == (4, 4, 1)


def swap_along(array, axis_name, partner):
    size = lax.axis_size(axis_name)
    return lax.ppermute(array, axis_name, [(i, i ^ partner) for i in range(size)])


def swaps_along(array, axis_name):
    return [swap_along(array, axis_name, partner) for partner in range(1, lax.axis_size(axis_name))]


def in_vmem(*arrays):
    return [pltpu.with_memory_space_constraint(array, pltpu.VMEM) for array in arrays]


def slot_of(index, width, count):
    slot = jnp.zeros_like(index)
    for bound in range(1, count):
        slot = slot + (index >= bound * width).astype(jnp.int32)
    return slot


def rows_of(slot):
    return pl.ds(pl.multiple_of(slot * HD, HD), HD)


def join_kernel(k_ref, v_ref, out_ref):
    width = k_ref.shape[1]
    out_ref[:, :width] = k_ref[...]
    out_ref[:, width:] = v_ref[...]


def prep_kernel(rows, nq, nz, mask_ref, doc_ref, q_ref, order_ref, *refs):
    *slot_refs, bias_ref = refs
    heads = mask_ref.shape[0]
    for slot in range(heads):
        order_ref[slot] = 0
    kept = jnp.int32(0)
    for head in range(heads):
        order_ref[kept] = head
        kept = kept + mask_ref[head]
    order_ref[heads] = kept
    slot = 0
    for ref in slot_refs:
        for place in range(ref.shape[0]):
            ref[place] = q_ref[:, rows_of(order_ref[slot])]
            slot += 1
    quarter = rows * nz
    total = quarter * nq
    q_at = lax.axis_index("qring")
    z_at = lax.axis_index("kvring")
    doc = doc_ref[...].reshape(1, total)
    row = lax.broadcasted_iota(jnp.int32, (quarter, 1), 0)
    row_z = slot_of(row, rows, nz)
    row_pos = q_at * quarter + (row_z ^ z_at) * rows + row - row_z * rows
    col = lax.broadcasted_iota(jnp.int32, (1, total), 1)
    col_q = slot_of(col, quarter, nq)
    rest = col - col_q * quarter
    col_z = slot_of(rest, rows, nz)
    col_pos = (col_q ^ q_at) * quarter + (col_z ^ z_at) * rows + rest - col_z * rows
    own_doc = jnp.sum(jnp.where(col == row_pos, doc, 0), axis=1, keepdims=True)
    first = jnp.sum((doc < own_doc).astype(jnp.int32), axis=1, keepdims=True)
    bias_ref[...] = jnp.where((col_pos >= first) & (col_pos <= row_pos), 0.0, NEG)


def kv_at(slot, kv_refs, order_ref, is_value):
    heads = order_ref.shape[0] - 1
    kv_heads = kv_refs[0].shape[1] // (2 * HD)
    group = order_ref[slot] // (heads // kv_heads) + is_value * kv_heads
    return jnp.concatenate([ref[:, rows_of(group)] for ref in kv_refs], axis=0)


def scores_of(q, slot, kv_refs, order_ref):
    k = kv_at(slot, kv_refs, order_ref, 0)
    return lax.dot_general(q, k, (((1,), (1,)), ((), ())), preferred_element_type=jnp.float32)


def attended(scores, bias, slot, kv_refs, order_ref):
    scores = scores * (LOG2E / math.sqrt(HD)) + bias
    weights = jnp.exp2(scores - jnp.max(scores, axis=1, keepdims=True))
    v = kv_at(slot, kv_refs, order_ref, 1)
    v_and_ones = jnp.concatenate([v, jnp.ones_like(v)], axis=1)
    sums = jnp.dot(weights.astype(jnp.bfloat16), v_and_ones, preferred_element_type=jnp.float32)
    keep = (slot < order_ref[order_ref.shape[0] - 1]).astype(jnp.float32)
    return (sums[:, :HD] * (keep / sums[:, HD:])).astype(jnp.bfloat16)


def own_kernel(nq, order_ref, *refs):
    kv_refs, (q_ref, bias_ref, att_ref) = refs[:nq], refs[nq:]
    rows = q_ref.shape[1]

    def one_slot(slot):
        scores = scores_of(q_ref[slot], slot, kv_refs, order_ref)
        att_ref[slot] = attended(scores, bias_ref[:rows], slot, kv_refs, order_ref)

    pl.loop(0, FAR_SLOTS, unroll=FAR_SLOTS // 2)(one_slot)


def first_kernel(nq, nz, order_ref, *refs):
    queries = nz * len(NEAR_SPLIT) + 1
    kv_refs, query_refs = refs[:nq], refs[nq : nq + queries]
    bias_ref, w_hbm, acc_ref, w_far_ref, w_ref, q_ref, att_ref, score_ref, sem = refs[nq + queries :]
    heads = order_ref.shape[0] - 1
    rest_slots = heads - FAR_SLOTS - NEAR_SLOTS
    kept = order_ref[heads]
    extra = jnp.clip((kept - FAR_SLOTS - NEAR_SLOTS + PAIR - 1) // PAIR, 0, rest_slots // PAIR)
    pairs = NEAR_SLOTS // PAIR + extra

    def near_copy(slot):
        return pltpu.make_async_copy(
            w_hbm.at[rows_of(order_ref[FAR_SLOTS + slot])], w_ref.at[rows_of(slot)], sem.at[slot]
        )

    def far_copy(slot):
        return pltpu.make_async_copy(
            w_hbm.at[rows_of(order_ref[slot])], w_far_ref.at[rows_of(slot)], sem.at[heads - FAR_SLOTS + slot]
        )

    pl.loop(0, pairs * PAIR)(lambda slot: near_copy(slot).start())
    pl.loop(0, FAR_SLOTS)(lambda slot: far_copy(slot).start())
    def place_rows(start, part_refs):
        for slot in range(part_refs[0].shape[0]):
            q_ref[start + slot] = jnp.concatenate([ref[slot] for ref in part_refs], axis=0)

    start = 0
    for index, slots in enumerate(NEAR_SPLIT):
        place_rows(start, query_refs[index * nz : (index + 1) * nz])
        start += slots
    rest_refs = [query_refs[-1].at[part * rest_slots : (part + 1) * rest_slots] for part in range(nz)]
    pl.when(extra > 0)(lambda: place_rows(start, rest_refs))

    def score(pair, place):
        slot = pair * PAIR + place
        score_ref[place] = scores_of(q_ref[slot], FAR_SLOTS + slot, kv_refs, order_ref)

    def project(pair):
        rows = pl.ds(pl.multiple_of(pair * PAIR * HD, HD), PAIR * HD)
        for at in range(0, acc_ref.shape[1], TILE):
            acc_ref[:, at : at + TILE] += jnp.dot(
                att_ref[...], w_ref[rows, at : at + TILE], preferred_element_type=jnp.float32
            )

    acc_ref[...] = jnp.zeros_like(acc_ref)
    att_ref[...] = jnp.zeros_like(att_ref)
    for place in range(PAIR):
        score(0, place)
        near_copy(place).wait()

    def one_pair(pair):
        later = jnp.minimum(pair + 1, pairs - 1)
        project(jnp.maximum(pair - 1, 0))
        for place in range(PAIR):
            slot = pair * PAIR + place
            att_ref[:, place * HD : (place + 1) * HD] = attended(
                score_ref[place], bias_ref[...], FAR_SLOTS + slot, kv_refs, order_ref
            )
            score(later, place)

        @pl.when(pair + 1 < pairs)
        def _():
            for place in range(PAIR):
                near_copy((pair + 1) * PAIR + place).wait()

    pl.loop(0, pairs)(one_pair)
    project(pairs - 1)
    pl.loop(0, FAR_SLOTS)(lambda slot: far_copy(slot).wait())


def last_kernel(nz, *refs):
    att_refs, (w_ref, acc_ref, out_ref, att_ref) = refs[:nz], refs[nz:]
    for slot in range(FAR_SLOTS):
        att_ref[:, slot * HD : (slot + 1) * HD] = jnp.concatenate([ref[slot] for ref in att_refs], axis=0)
    rows = att_refs[0].shape[1]
    z_at = lax.axis_index("kvring")
    for at in range(0, acc_ref.shape[1], TILE):
        mixed = acc_ref[:, at : at + TILE] + jnp.dot(
            att_ref[...], w_ref[:, at : at + TILE], preferred_element_type=jnp.float32
        )
        mixed = mixed.astype(jnp.bfloat16)
        for slot in range(nz):
            place = pl.multiple_of((z_at ^ slot) * rows, rows)
            out_ref[pl.ds(place, rows), at : at + TILE] = mixed[slot * rows : (slot + 1) * rows]


def per_device_small_ring(queries, keys, values, doc_ids, head_mask, w_out):
    rows = queries.shape[0]
    nq = lax.axis_size("qring")
    nz = lax.axis_size("kvring")
    heads = head_mask.shape[0]
    width = w_out.shape[1]
    quarter = rows * nz
    total = quarter * nq
    rest_slots = heads - FAR_SLOTS - NEAR_SLOTS
    smem = pl.BlockSpec(memory_space=pltpu.SMEM)
    vmem = pl.BlockSpec(memory_space=pltpu.VMEM)
    hbm = pl.BlockSpec(memory_space=pl.ANY)
    params = pltpu.CompilerParams(vmem_limit_bytes=VMEM_LIMIT)

    def cost(micros):
        return pl.CostEstimate(flops=int(micros * 1e9), bytes_accessed=0, transcendentals=0)

    def slots_in_vmem(slots):
        return pltpu.VMEM((slots, rows, HD), jnp.bfloat16)

    kv_own = pl.pallas_call(
        join_kernel,
        out_shape=pltpu.VMEM((rows, 2 * keys.shape[1]), jnp.bfloat16),
        in_specs=[vmem, vmem],
        out_specs=vmem,
        name="join",
    )(keys, values)
    kv_parts = [kv_own, *swaps_along(kv_own, "kvring")]
    order, far, *near, rest, bias = pl.pallas_call(
        functools.partial(prep_kernel, rows, nq, nz),
        out_shape=(
            jax.ShapeDtypeStruct((heads + 1,), jnp.int32),
            *(slots_in_vmem(slots) for slots in (FAR_SLOTS, *NEAR_SPLIT, rest_slots)),
            pltpu.VMEM((quarter, total), jnp.float32),
        ),
        in_specs=[smem, vmem, vmem],
        out_specs=[smem] + [vmem] * (len(NEAR_SPLIT) + 3),
        cost_estimate=cost(4),
        name="prep",
    )(head_mask, doc_ids, queries)
    many = jnp.sum(head_mask) > NEAR_SLOTS + FAR_SLOTS
    *kv_parts, near[0], near[1], order, many = lax.optimization_barrier((*kv_parts, *near, order, many))
    kv0 = jnp.concatenate(kv_parts, axis=0)
    kv2 = swap_along(kv0, "qring", 2)
    near_parts = [[array, *swaps_along(array, "kvring")] for array in near]
    rest_all = lax.cond(
        many,
        lambda array: jnp.concatenate([array, *swaps_along(array, "kvring")]),
        lambda array: jnp.zeros((nz * rest_slots, rows, HD), array.dtype),
        lax.optimization_barrier((rest, kv0))[0],
    )
    kv0, rest_all, *near_parts[0] = lax.optimization_barrier((kv0, rest_all, *near_parts[0]))
    kv1 = swap_along(kv0, "qring", 1)
    kv3 = swap_along(kv2, "qring", 1)
    kv = (kv0, kv1, kv2, kv3)
    far_own = pl.pallas_call(
        functools.partial(own_kernel, nq),
        out_shape=slots_in_vmem(FAR_SLOTS),
        in_specs=[smem] + [vmem] * (nq + 2),
        out_specs=vmem,
        compiler_params=params,
        cost_estimate=cost(2),
        name="own",
    )(order, *in_vmem(*kv, far, bias))
    far_parts = [far_own, *swaps_along(far_own, "kvring")]
    acc, w_far = pl.pallas_call(
        functools.partial(first_kernel, nq, nz),
        out_shape=(
            pltpu.VMEM((quarter, width), jnp.float32),
            pltpu.VMEM((FAR_SLOTS * HD, width), jnp.bfloat16),
        ),
        in_specs=[smem] + [vmem] * (nq + nz * len(near) + 2) + [hbm],
        out_specs=(vmem, vmem),
        scratch_shapes=[
            pltpu.VMEM(((heads - FAR_SLOTS) * HD, width), jnp.bfloat16),
            pltpu.VMEM((heads - FAR_SLOTS, quarter, HD), jnp.bfloat16),
            pltpu.VMEM((quarter, PAIR * HD), jnp.bfloat16),
            pltpu.VMEM((PAIR, quarter, total), jnp.float32),
            pltpu.SemaphoreType.DMA((heads,)),
        ],
        compiler_params=params,
        cost_estimate=cost(6),
        name="first",
    )(order, *in_vmem(*kv, *sum(near_parts, []), rest_all, bias), w_out)
    return pl.pallas_call(
        functools.partial(last_kernel, nz),
        out_shape=jax.ShapeDtypeStruct((quarter, width), jnp.bfloat16),
        in_specs=[vmem] * (nz + 2),
        out_specs=vmem,
        scratch_shapes=[pltpu.VMEM((quarter, FAR_SLOTS * HD), jnp.bfloat16)],
        compiler_params=params,
        name="last",
    )(*in_vmem(*far_parts, w_far, acc))


def solution(mesh):
    placed = (
        P(("groups", "qring", "kvring"), "head"),
        P(("groups", "qring", "kvring"), "head"),
        P(("groups", "qring", "kvring"), "head"),
        P("groups"),
        P("head"),
        P("head", "kvring"),
    )
    per_device = per_device_small_ring if small_ring(mesh) else per_device_any_ring
    return jax.shard_map(
        per_device,
        mesh=mesh,
        in_specs=placed,
        out_specs=P(("groups", "qring", "head"), "kvring"),
        check_vma=False,
    )
```

```python
import functools
import math

import jax
import jax.numpy as jnp
from jax import lax
from jax.experimental import pallas as pl
from jax.experimental.pallas import tpu as pltpu
from jax.sharding import PartitionSpec as P

HD = 128


NEG = -1e30


def block_rows(total_rows, shard_rows):
    best_size = shard_rows
    for multiple in range(1, total_rows // shard_rows + 1):
        if total_rows // shard_rows % multiple == 0 and multiple * shard_rows <= 256:
            best_size = multiple * shard_rows
    return best_size


def attend_keys(state, visible, queries4, key_rows, value_rows, scale_factor):
    run_max, run_sum, run_out = state
    mask4 = visible[:, None, None, :]
    scores = (
        jnp.einsum("rgec,kgc->rgek", queries4, key_rows, preferred_element_type=jnp.float32)
        * scale_factor
    )
    scores = jnp.where(mask4, scores, NEG)
    new_max = jnp.maximum(run_max, jnp.max(scores, axis=-1))
    weights = jnp.where(mask4, jnp.exp(scores - new_max[..., None]), 0.0)
    shrink = jnp.exp(run_max - new_max)
    run_sum = run_sum * shrink + jnp.sum(weights, axis=-1)
    update = jnp.einsum(
        "rgek,kgc->rgec",
        weights.astype(jnp.bfloat16),
        value_rows,
        preferred_element_type=jnp.float32,
    )
    run_out = run_out * shrink[..., None] + update
    return (new_max, run_sum, run_out)


def fold_piece(
    state, pieces, key_start, queries4, query_doc, query_pos, doc_ids, shard_rows, scale_factor
):
    key_all, value_all = pieces
    total_rows = key_all.shape[0]
    block_size = block_rows(total_rows, shard_rows)

    def one_block(index, carry):
        offset = index * block_size
        key_rows = lax.dynamic_slice_in_dim(key_all, offset, block_size, 0)
        value_rows = lax.dynamic_slice_in_dim(value_all, offset, block_size, 0)
        first = key_start + offset
        key_doc = lax.dynamic_slice_in_dim(doc_ids, first, block_size, 0)
        key_pos = first + jnp.arange(block_size, dtype=jnp.int32)
        visible = (query_doc[:, None] == key_doc[None, :]) & (
            key_pos[None, :] <= query_pos[:, None]
        )
        return attend_keys(carry, visible, queries4, key_rows, value_rows, scale_factor)

    return lax.fori_loop(0, total_rows // block_size, one_block, state)


def per_device_any_ring(queries, keys, values, doc_ids, head_mask, w_out):
    shard_rows = queries.shape[0]
    kv_local = keys.shape[1] // HD
    q_local = queries.shape[1] // HD
    per_group = q_local // kv_local
    scale_factor = 1.0 / math.sqrt(HD)
    cycle_size = lax.axis_size("kvring")
    cycle_index = lax.axis_index("kvring")
    loop_index = lax.axis_index("qring")
    quarter = cycle_size * shard_rows
    key_rows = keys.reshape(shard_rows, kv_local, HD)
    value_rows = values.reshape(shard_rows, kv_local, HD)
    loop_size = lax.axis_size("qring")
    gathered = lax.all_gather(queries, "qring", axis=0, tiled=True)
    query_total = loop_size * shard_rows
    row_ids = jnp.arange(query_total, dtype=jnp.int32)
    query_pos = row_ids // shard_rows * quarter + cycle_index * shard_rows + row_ids % shard_rows
    queries4 = gathered.reshape(query_total, kv_local, per_group, HD)
    query_doc = jnp.take(doc_ids, query_pos)
    key_base = loop_index * quarter
    initial = (
        jnp.full((query_total, kv_local, per_group), NEG, jnp.float32),
        jnp.zeros((query_total, kv_local, per_group), jnp.float32),
        jnp.zeros((query_total, kv_local, per_group, HD), jnp.float32),
    )
    run_max, run_sum, run_out = fold_piece(
        initial,
        (
            lax.all_gather(key_rows, "kvring", axis=0, tiled=True),
            lax.all_gather(value_rows, "kvring", axis=0, tiled=True),
        ),
        key_base,
        queries4,
        query_doc,
        query_pos,
        doc_ids,
        shard_rows,
        scale_factor,
    )
    top = lax.pmax(run_max, "qring")
    factor = jnp.exp(run_max - top)
    numer, denom = (
        lax.psum_scatter(
            (run_out * factor[..., None]).astype(jnp.bfloat16),
            "qring",
            scatter_dimension=0,
            tiled=True,
        ).astype(jnp.float32),
        lax.psum_scatter(
            (run_sum * factor).astype(jnp.bfloat16), "qring", scatter_dimension=0, tiled=True
        ).astype(jnp.float32),
    )
    mask_f = head_mask.reshape(kv_local, per_group).astype(jnp.float32)
    attended = (
        (numer / denom[..., None] * mask_f[None, :, :, None])
        .astype(jnp.bfloat16)
        .reshape(shard_rows, q_local * HD)
    )
    partial_sum = jnp.dot(
        lax.all_gather(attended, "kvring", axis=0, tiled=True),
        w_out,
        preferred_element_type=jnp.float32,
    )
    return lax.psum_scatter(
        partial_sum.astype(jnp.bfloat16), "head", scatter_dimension=0, tiled=True
    )


VMEM_LIMIT = 32 * 1024 * 1024
LOG2E = math.log2(math.e)
PAIR = 2
NEAR_SPLIT = (8, 8)
NEAR_SLOTS = sum(NEAR_SPLIT)
FAR_SLOTS = 10
TILE = 1024


def small_ring(mesh):
    return (mesh.shape["qring"], mesh.shape["kvring"], mesh.shape["head"]) == (4, 4, 1)


def swap_along(array, axis_name, partner):
    size = lax.axis_size(axis_name)
    return lax.ppermute(array, axis_name, [(i, i ^ partner) for i in range(size)])


def partner_of(slot, count):
    return (count - slot) % count


def swaps_along(array, axis_name):
    size = lax.axis_size(axis_name)
    return [swap_along(array, axis_name, partner_of(slot, size)) for slot in range(1, size)]


def in_vmem(*arrays):
    return [pltpu.with_memory_space_constraint(array, pltpu.VMEM) for array in arrays]


def slot_of(index, width, count):
    slot = jnp.zeros_like(index)
    for bound in range(1, count):
        slot = slot + (index >= bound * width).astype(jnp.int32)
    return slot


def rows_of(slot):
    return pl.ds(pl.multiple_of(slot * HD, HD), HD)


def join_kernel(k_ref, v_ref, out_ref):
    width = k_ref.shape[1]
    out_ref[:, :width] = k_ref[...]
    out_ref[:, width:] = v_ref[...]


def prep_kernel(rows, nq, nz, mask_ref, doc_ref, q_ref, order_ref, *refs):
    *slot_refs, bias_ref = refs
    heads = mask_ref.shape[0]
    for slot in range(heads):
        order_ref[slot] = 0
    kept = jnp.int32(0)
    for head in range(heads):
        order_ref[kept] = head
        kept = kept + mask_ref[head]
    order_ref[heads] = kept
    slot = 0
    for ref in slot_refs:
        for place in range(ref.shape[0]):
            ref[place] = q_ref[:, rows_of(order_ref[slot])]
            slot += 1
    quarter = rows * nz
    total = quarter * nq
    q_at = lax.axis_index("qring")
    z_at = lax.axis_index("kvring")
    doc = doc_ref[...].reshape(1, total)
    row = lax.broadcasted_iota(jnp.int32, (quarter, 1), 0)
    row_z = slot_of(row, rows, nz)
    row_pos = q_at * quarter + (partner_of(row_z, nz) ^ z_at) * rows + row - row_z * rows
    col = lax.broadcasted_iota(jnp.int32, (1, total), 1)
    col_q = slot_of(col, quarter, nq)
    rest = col - col_q * quarter
    col_z = slot_of(rest, rows, nz)
    col_pos = (((col_q & 1) * 2 + (col_q >> 1)) ^ q_at) * quarter + (partner_of(col_z, nz) ^ z_at) * rows + rest - col_z * rows
    own_doc = jnp.sum(jnp.where(col == row_pos, doc, 0), axis=1, keepdims=True)
    first = jnp.sum((doc < own_doc).astype(jnp.int32), axis=1, keepdims=True)
    bias_ref[...] = jnp.where((col_pos >= first) & (col_pos <= row_pos), 0.0, NEG)


def kv_at(slot, kv_refs, order_ref, is_value):
    heads = order_ref.shape[0] - 1
    kv_heads = kv_refs[0].shape[1] // (2 * HD)
    group = order_ref[slot] // (heads // kv_heads) + is_value * kv_heads
    return jnp.concatenate([ref[:, rows_of(group)] for ref in kv_refs], axis=0)


def scores_of(q, slot, kv_refs, order_ref):
    k = kv_at(slot, kv_refs, order_ref, 0)
    return lax.dot_general(q, k, (((1,), (1,)), ((), ())), preferred_element_type=jnp.float32)


def attended(scores, bias, slot, kv_refs, order_ref):
    scores = scores * (LOG2E / math.sqrt(HD)) + bias
    weights = jnp.exp2(scores - jnp.max(scores, axis=1, keepdims=True))
    v = kv_at(slot, kv_refs, order_ref, 1)
    v_and_ones = jnp.concatenate([v, jnp.ones_like(v)], axis=1)
    sums = jnp.dot(weights.astype(jnp.bfloat16), v_and_ones, preferred_element_type=jnp.float32)
    keep = (slot < order_ref[order_ref.shape[0] - 1]).astype(jnp.float32)
    return (sums[:, :HD] * (keep / sums[:, HD:])).astype(jnp.bfloat16)


def own_kernel(kvs, order_ref, *refs):
    kv_refs, (q_ref, bias_ref, att_ref) = refs[:kvs], refs[kvs:]
    rows = q_ref.shape[1]

    def one_slot(slot):
        scores = scores_of(q_ref[slot], slot, kv_refs, order_ref)
        att_ref[slot] = attended(scores, bias_ref[:rows], slot, kv_refs, order_ref)

    pl.loop(0, FAR_SLOTS, unroll=FAR_SLOTS // 2)(one_slot)


def first_kernel(kvs, nz, order_ref, *refs):
    queries = nz * len(NEAR_SPLIT) + 1
    kv_refs, query_refs = refs[:kvs], refs[kvs : kvs + queries]
    bias_ref, w_hbm, acc_ref, w_far_ref, w_ref, q_ref, att_ref, score_ref, sem = refs[kvs + queries :]
    heads = order_ref.shape[0] - 1
    rest_slots = heads - FAR_SLOTS - NEAR_SLOTS
    kept = order_ref[heads]
    extra = jnp.clip((kept - FAR_SLOTS - NEAR_SLOTS + PAIR - 1) // PAIR, 0, rest_slots // PAIR)
    pairs = NEAR_SLOTS // PAIR + extra

    def near_copy(slot):
        return pltpu.make_async_copy(
            w_hbm.at[rows_of(order_ref[FAR_SLOTS + slot])], w_ref.at[rows_of(slot)], sem.at[slot]
        )

    def far_copy(slot):
        return pltpu.make_async_copy(
            w_hbm.at[rows_of(order_ref[slot])], w_far_ref.at[rows_of(slot)], sem.at[heads - FAR_SLOTS + slot]
        )

    pl.loop(0, pairs * PAIR)(lambda slot: near_copy(slot).start())
    pl.loop(0, FAR_SLOTS)(lambda slot: far_copy(slot).start())
    def place_rows(start, part_refs):
        for slot in range(part_refs[0].shape[0]):
            q_ref[start + slot] = jnp.concatenate([ref[slot] for ref in part_refs], axis=0)

    start = 0
    for index, slots in enumerate(NEAR_SPLIT):
        place_rows(start, query_refs[index * nz : (index + 1) * nz])
        start += slots
    rest_refs = [query_refs[-1].at[part * rest_slots : (part + 1) * rest_slots] for part in range(nz)]
    pl.when(extra > 0)(lambda: place_rows(start, rest_refs))

    def score(pair, place):
        slot = pair * PAIR + place
        score_ref[place] = scores_of(q_ref[slot], FAR_SLOTS + slot, kv_refs, order_ref)

    def project(pair):
        rows = pl.ds(pl.multiple_of(pair * PAIR * HD, HD), PAIR * HD)
        for at in range(0, acc_ref.shape[1], TILE):
            acc_ref[:, at : at + TILE] += jnp.dot(
                att_ref[...], w_ref[rows, at : at + TILE], preferred_element_type=jnp.float32
            )

    acc_ref[...] = jnp.zeros_like(acc_ref)
    att_ref[...] = jnp.zeros_like(att_ref)
    for place in range(PAIR):
        score(0, place)
        near_copy(place).wait()

    def one_pair(pair):
        later = jnp.minimum(pair + 1, pairs - 1)
        project(jnp.maximum(pair - 1, 0))
        for place in range(PAIR):
            slot = pair * PAIR + place
            att_ref[:, place * HD : (place + 1) * HD] = attended(
                score_ref[place], bias_ref[...], FAR_SLOTS + slot, kv_refs, order_ref
            )
            score(later, place)

        @pl.when(pair + 1 < pairs)
        def _():
            for place in range(PAIR):
                near_copy((pair + 1) * PAIR + place).wait()

    pl.loop(0, pairs)(one_pair)
    project(pairs - 1)
    pl.loop(0, FAR_SLOTS)(lambda slot: far_copy(slot).wait())


def last_kernel(nz, *refs):
    att_refs, (w_ref, acc_ref, out_ref, att_ref) = refs[:nz], refs[nz:]
    for slot in range(FAR_SLOTS):
        att_ref[:, slot * HD : (slot + 1) * HD] = jnp.concatenate([ref[slot] for ref in att_refs], axis=0)
    rows = att_refs[0].shape[1]
    z_at = lax.axis_index("kvring")
    for at in range(0, acc_ref.shape[1], TILE):
        mixed = acc_ref[:, at : at + TILE] + jnp.dot(
            att_ref[...], w_ref[:, at : at + TILE], preferred_element_type=jnp.float32
        )
        mixed = mixed.astype(jnp.bfloat16)
        for slot in range(nz):
            place = pl.multiple_of((z_at ^ partner_of(slot, nz)) * rows, rows)
            out_ref[pl.ds(place, rows), at : at + TILE] = mixed[slot * rows : (slot + 1) * rows]


def per_device_small_ring(queries, keys, values, doc_ids, head_mask, w_out):
    rows = queries.shape[0]
    nq = lax.axis_size("qring")
    nz = lax.axis_size("kvring")
    heads = head_mask.shape[0]
    width = w_out.shape[1]
    quarter = rows * nz
    total = quarter * nq
    rest_slots = heads - FAR_SLOTS - NEAR_SLOTS
    smem = pl.BlockSpec(memory_space=pltpu.SMEM)
    vmem = pl.BlockSpec(memory_space=pltpu.VMEM)
    hbm = pl.BlockSpec(memory_space=pl.ANY)
    params = pltpu.CompilerParams(vmem_limit_bytes=VMEM_LIMIT)

    def cost(micros):
        return pl.CostEstimate(flops=int(micros * 1e9), bytes_accessed=0, transcendentals=0)

    def slots_in_vmem(slots):
        return pltpu.VMEM((slots, rows, HD), jnp.bfloat16)

    kv_own = pl.pallas_call(
        join_kernel,
        out_shape=pltpu.VMEM((rows, 2 * keys.shape[1]), jnp.bfloat16),
        in_specs=[vmem, vmem],
        out_specs=vmem,
        name="join",
    )(keys, values)
    kv_parts = [kv_own, *swaps_along(kv_own, "kvring")]
    order, far, *near, rest, bias = pl.pallas_call(
        functools.partial(prep_kernel, rows, nq, nz),
        out_shape=(
            pltpu.SMEM((heads + 1,), jnp.int32),
            *(slots_in_vmem(slots) for slots in (FAR_SLOTS, *NEAR_SPLIT, rest_slots)),
            pltpu.VMEM((quarter, total), jnp.float32),
        ),
        in_specs=[smem, vmem, vmem],
        out_specs=[smem] + [vmem] * (len(NEAR_SPLIT) + 3),
        cost_estimate=cost(4),
        name="prep",
    )(head_mask, doc_ids, queries)
    many = jnp.sum(head_mask) > NEAR_SLOTS + FAR_SLOTS
    *kv_parts, near[0], near[1], order, many = lax.optimization_barrier((*kv_parts, *near, order, many))
    kv0 = jnp.concatenate(kv_parts, axis=0)
    kv2 = swap_along(kv0, "qring", 2)
    near_parts = [[array, *swaps_along(array, "kvring")] for array in near]
    rest_all = lax.cond(
        many,
        lambda array: jnp.concatenate([array, *swaps_along(array, "kvring")]),
        lambda array: jnp.zeros((nz * rest_slots, rows, HD), array.dtype),
        lax.optimization_barrier((rest, kv0))[0],
    )
    *near_parts[0], kv2, rest_all = lax.optimization_barrier((*near_parts[0], kv2, rest_all))
    kv02 = jnp.concatenate([kv0, kv2], axis=0)
    kv = (kv02, swap_along(kv02, "qring", 1))
    far_own = pl.pallas_call(
        functools.partial(own_kernel, len(kv)),
        out_shape=slots_in_vmem(FAR_SLOTS),
        in_specs=[smem] + [vmem] * (len(kv) + 2),
        out_specs=vmem,
        compiler_params=params,
        cost_estimate=cost(2),
        name="own",
    )(order, *in_vmem(*kv, far, bias))
    far_parts = [far_own, *swaps_along(far_own, "kvring")]
    acc, w_far = pl.pallas_call(
        functools.partial(first_kernel, len(kv), nz),
        out_shape=(
            pltpu.VMEM((quarter, width), jnp.float32),
            pltpu.VMEM((FAR_SLOTS * HD, width), jnp.bfloat16),
        ),
        in_specs=[smem] + [vmem] * (len(kv) + nz * len(near) + 2) + [hbm],
        out_specs=(vmem, vmem),
        scratch_shapes=[
            pltpu.VMEM(((heads - FAR_SLOTS) * HD, width), jnp.bfloat16),
            pltpu.VMEM((heads - FAR_SLOTS, quarter, HD), jnp.bfloat16),
            pltpu.VMEM((quarter, PAIR * HD), jnp.bfloat16),
            pltpu.VMEM((PAIR, quarter, total), jnp.float32),
            pltpu.SemaphoreType.DMA((heads,)),
        ],
        compiler_params=params,
        cost_estimate=cost(6),
        name="first",
    )(order, *in_vmem(*kv, *sum(near_parts, []), rest_all, bias), w_out)
    return pl.pallas_call(
        functools.partial(last_kernel, nz),
        out_shape=jax.ShapeDtypeStruct((quarter, width), jnp.bfloat16),
        in_specs=[vmem] * (nz + 2),
        out_specs=vmem,
        scratch_shapes=[pltpu.VMEM((quarter, FAR_SLOTS * HD), jnp.bfloat16)],
        compiler_params=params,
        name="last",
    )(*in_vmem(*far_parts, w_far, acc))


def solution(mesh):
    placed = (
        P(("groups", "qring", "kvring"), "head"),
        P(("groups", "qring", "kvring"), "head"),
        P(("groups", "qring", "kvring"), "head"),
        P("groups"),
        P("head"),
        P("head", "kvring"),
    )
    per_device = per_device_small_ring if small_ring(mesh) else per_device_any_ring
    return jax.shard_map(
        per_device,
        mesh=mesh,
        in_specs=placed,
        out_specs=P(("groups", "qring", "head"), "kvring"),
        check_vma=False,
    )
```

```python
import functools
import math

import jax
import jax.numpy as jnp
from jax import lax
from jax.experimental import pallas as pl
from jax.experimental.pallas import tpu as pltpu
from jax.sharding import PartitionSpec as P

HD = 128


NEG = -1e30


def block_rows(total_rows, shard_rows):
    best_size = shard_rows
    for multiple in range(1, total_rows // shard_rows + 1):
        if total_rows // shard_rows % multiple == 0 and multiple * shard_rows <= 256:
            best_size = multiple * shard_rows
    return best_size


def attend_keys(state, visible, queries4, key_rows, value_rows, scale_factor):
    run_max, run_sum, run_out = state
    mask4 = visible[:, None, None, :]
    scores = (
        jnp.einsum("rgec,kgc->rgek", queries4, key_rows, preferred_element_type=jnp.float32)
        * scale_factor
    )
    scores = jnp.where(mask4, scores, NEG)
    new_max = jnp.maximum(run_max, jnp.max(scores, axis=-1))
    weights = jnp.where(mask4, jnp.exp(scores - new_max[..., None]), 0.0)
    shrink = jnp.exp(run_max - new_max)
    run_sum = run_sum * shrink + jnp.sum(weights, axis=-1)
    update = jnp.einsum(
        "rgek,kgc->rgec",
        weights.astype(jnp.bfloat16),
        value_rows,
        preferred_element_type=jnp.float32,
    )
    run_out = run_out * shrink[..., None] + update
    return (new_max, run_sum, run_out)


def fold_piece(
    state, pieces, key_start, queries4, query_doc, query_pos, doc_ids, shard_rows, scale_factor
):
    key_all, value_all = pieces
    total_rows = key_all.shape[0]
    block_size = block_rows(total_rows, shard_rows)

    def one_block(index, carry):
        offset = index * block_size
        key_rows = lax.dynamic_slice_in_dim(key_all, offset, block_size, 0)
        value_rows = lax.dynamic_slice_in_dim(value_all, offset, block_size, 0)
        first = key_start + offset
        key_doc = lax.dynamic_slice_in_dim(doc_ids, first, block_size, 0)
        key_pos = first + jnp.arange(block_size, dtype=jnp.int32)
        visible = (query_doc[:, None] == key_doc[None, :]) & (
            key_pos[None, :] <= query_pos[:, None]
        )
        return attend_keys(carry, visible, queries4, key_rows, value_rows, scale_factor)

    return lax.fori_loop(0, total_rows // block_size, one_block, state)


def per_device_any_ring(queries, keys, values, doc_ids, head_mask, w_out):
    shard_rows = queries.shape[0]
    kv_local = keys.shape[1] // HD
    q_local = queries.shape[1] // HD
    per_group = q_local // kv_local
    scale_factor = 1.0 / math.sqrt(HD)
    cycle_size = lax.axis_size("kvring")
    cycle_index = lax.axis_index("kvring")
    loop_index = lax.axis_index("qring")
    quarter = cycle_size * shard_rows
    key_rows = keys.reshape(shard_rows, kv_local, HD)
    value_rows = values.reshape(shard_rows, kv_local, HD)
    loop_size = lax.axis_size("qring")
    gathered = lax.all_gather(queries, "qring", axis=0, tiled=True)
    query_total = loop_size * shard_rows
    row_ids = jnp.arange(query_total, dtype=jnp.int32)
    query_pos = row_ids // shard_rows * quarter + cycle_index * shard_rows + row_ids % shard_rows
    queries4 = gathered.reshape(query_total, kv_local, per_group, HD)
    query_doc = jnp.take(doc_ids, query_pos)
    key_base = loop_index * quarter
    initial = (
        jnp.full((query_total, kv_local, per_group), NEG, jnp.float32),
        jnp.zeros((query_total, kv_local, per_group), jnp.float32),
        jnp.zeros((query_total, kv_local, per_group, HD), jnp.float32),
    )
    run_max, run_sum, run_out = fold_piece(
        initial,
        (
            lax.all_gather(key_rows, "kvring", axis=0, tiled=True),
            lax.all_gather(value_rows, "kvring", axis=0, tiled=True),
        ),
        key_base,
        queries4,
        query_doc,
        query_pos,
        doc_ids,
        shard_rows,
        scale_factor,
    )
    top = lax.pmax(run_max, "qring")
    factor = jnp.exp(run_max - top)
    numer, denom = (
        lax.psum_scatter(
            (run_out * factor[..., None]).astype(jnp.bfloat16),
            "qring",
            scatter_dimension=0,
            tiled=True,
        ).astype(jnp.float32),
        lax.psum_scatter(
            (run_sum * factor).astype(jnp.bfloat16), "qring", scatter_dimension=0, tiled=True
        ).astype(jnp.float32),
    )
    mask_f = head_mask.reshape(kv_local, per_group).astype(jnp.float32)
    attended = (
        (numer / denom[..., None] * mask_f[None, :, :, None])
        .astype(jnp.bfloat16)
        .reshape(shard_rows, q_local * HD)
    )
    partial_sum = jnp.dot(
        lax.all_gather(attended, "kvring", axis=0, tiled=True),
        w_out,
        preferred_element_type=jnp.float32,
    )
    return lax.psum_scatter(
        partial_sum.astype(jnp.bfloat16), "head", scatter_dimension=0, tiled=True
    )


VMEM_LIMIT = 32 * 1024 * 1024
LOG2E = math.log2(math.e)
PAIR = 2
NEAR_SLOTS = 14
EARLY = (1,)
FAR_SLOTS = 12
TILE = 1024


def small_ring(mesh):
    return (mesh.shape["qring"], mesh.shape["kvring"], mesh.shape["head"]) == (4, 4, 1)


def swap_along(array, axis_name, partner):
    size = lax.axis_size(axis_name)
    return lax.ppermute(array, axis_name, [(i, i ^ partner) for i in range(size)])


def partner_of(slot, count):
    return (count - slot) % count


def swaps_along(array, axis_name):
    size = lax.axis_size(axis_name)
    return [swap_along(array, axis_name, partner_of(slot, size)) for slot in range(1, size)]


def in_vmem(*arrays):
    return [pltpu.with_memory_space_constraint(array, pltpu.VMEM) for array in arrays]


def slot_of(index, width, count):
    slot = jnp.zeros_like(index)
    for bound in range(1, count):
        slot = slot + (index >= bound * width).astype(jnp.int32)
    return slot


def rows_of(slot):
    return pl.ds(pl.multiple_of(slot * HD, HD), HD)


def join_kernel(k_ref, v_ref, out_ref):
    width = k_ref.shape[1]
    out_ref[:, :width] = k_ref[...]
    out_ref[:, width:] = v_ref[...]


def prep_kernel(rows, nq, nz, mask_ref, doc_ref, q_ref, order_ref, *refs):
    *slot_refs, bias_ref = refs
    heads = mask_ref.shape[0]
    for slot in range(heads):
        order_ref[slot] = 0
    kept = jnp.int32(0)
    for head in range(heads):
        order_ref[kept] = head
        kept = kept + mask_ref[head]
    order_ref[heads] = kept
    slot = 0
    for ref in slot_refs:
        for place in range(ref.shape[0]):
            ref[place] = q_ref[:, rows_of(order_ref[slot])]
            slot += 1
    quarter = rows * nz
    total = quarter * nq
    q_at = lax.axis_index("qring")
    z_at = lax.axis_index("kvring")
    doc = doc_ref[...].reshape(1, total)
    row = lax.broadcasted_iota(jnp.int32, (quarter, 1), 0)
    row_z = slot_of(row, rows, nz)
    row_pos = q_at * quarter + (partner_of(row_z, nz) ^ z_at) * rows + row - row_z * rows
    col = lax.broadcasted_iota(jnp.int32, (1, total), 1)
    col_q = slot_of(col, quarter, nq)
    rest = col - col_q * quarter
    col_z = slot_of(rest, rows, nz)
    col_pos = (((col_q & 1) * 2 + (col_q >> 1)) ^ q_at) * quarter + (partner_of(col_z, nz) ^ z_at) * rows + rest - col_z * rows
    own_doc = jnp.sum(jnp.where(col == row_pos, doc, 0), axis=1, keepdims=True)
    first = jnp.sum((doc < own_doc).astype(jnp.int32), axis=1, keepdims=True)
    bias_ref[...] = jnp.where((col_pos >= first) & (col_pos <= row_pos), 0.0, NEG)


def kv_at(slot, kv_refs, order_ref, is_value):
    heads = order_ref.shape[0] - 1
    kv_heads = kv_refs[0].shape[1] // (2 * HD)
    group = order_ref[slot] // (heads // kv_heads) + is_value * kv_heads
    return jnp.concatenate([ref[:, rows_of(group)] for ref in kv_refs], axis=0)


def scores_of(q, slot, kv_refs, order_ref):
    k = kv_at(slot, kv_refs, order_ref, 0)
    return lax.dot_general(q, k, (((1,), (1,)), ((), ())), preferred_element_type=jnp.float32)


def attended(scores, bias, slot, kv_refs, order_ref):
    scores = scores * (LOG2E / math.sqrt(HD)) + bias
    weights = jnp.exp2(scores - jnp.max(scores, axis=1, keepdims=True))
    v = kv_at(slot, kv_refs, order_ref, 1)
    v_and_ones = jnp.concatenate([v, jnp.ones_like(v)], axis=1)
    sums = jnp.dot(weights.astype(jnp.bfloat16), v_and_ones, preferred_element_type=jnp.float32)
    keep = (slot < order_ref[order_ref.shape[0] - 1]).astype(jnp.float32)
    return (sums[:, :HD] * (keep / sums[:, HD:])).astype(jnp.bfloat16)


def own_kernel(kvs, order_ref, *refs):
    kv_refs, (q_ref, bias_ref, att_ref) = refs[:kvs], refs[kvs:]
    rows = q_ref.shape[1]

    def one_slot(slot):
        scores = scores_of(q_ref[slot], slot, kv_refs, order_ref)
        att_ref[slot] = attended(scores, bias_ref[:rows], slot, kv_refs, order_ref)

    pl.loop(0, FAR_SLOTS, unroll=FAR_SLOTS // 2)(one_slot)


def first_kernel(kvs, nz, order_ref, *refs):
    queries = nz + 1
    kv_refs, query_refs = refs[:kvs], refs[kvs : kvs + queries]
    bias_ref, w_hbm, acc_ref, w_far_ref, w_ref, q_ref, att_ref, score_ref, sem = refs[kvs + queries :]
    heads = order_ref.shape[0] - 1
    rest_slots = heads - FAR_SLOTS - NEAR_SLOTS
    kept = order_ref[heads]
    extra = jnp.clip((kept - FAR_SLOTS - NEAR_SLOTS + PAIR - 1) // PAIR, 0, rest_slots // PAIR)
    pairs = NEAR_SLOTS // PAIR + extra

    def near_copy(slot):
        return pltpu.make_async_copy(
            w_hbm.at[rows_of(order_ref[FAR_SLOTS + slot])], w_ref.at[rows_of(slot)], sem.at[slot]
        )

    def far_copy(slot):
        return pltpu.make_async_copy(
            w_hbm.at[rows_of(order_ref[slot])], w_far_ref.at[rows_of(slot)], sem.at[heads - FAR_SLOTS + slot]
        )

    pl.loop(0, pairs * PAIR)(lambda slot: near_copy(slot).start())
    pl.loop(0, FAR_SLOTS)(lambda slot: far_copy(slot).start())
    def place_rows(start, part_refs):
        for slot in range(part_refs[0].shape[0]):
            q_ref[start + slot] = jnp.concatenate([ref[slot] for ref in part_refs], axis=0)

    place_rows(0, query_refs[:nz])
    rest_refs = [query_refs[-1].at[part * rest_slots : (part + 1) * rest_slots] for part in range(nz)]
    pl.when(extra > 0)(lambda: place_rows(NEAR_SLOTS, rest_refs))

    def score(pair, place):
        slot = pair * PAIR + place
        score_ref[place] = scores_of(q_ref[slot], FAR_SLOTS + slot, kv_refs, order_ref)

    def project(pair):
        rows = pl.ds(pl.multiple_of(pair * PAIR * HD, HD), PAIR * HD)
        for at in range(0, acc_ref.shape[1], TILE):
            acc_ref[:, at : at + TILE] += jnp.dot(
                att_ref[...], w_ref[rows, at : at + TILE], preferred_element_type=jnp.float32
            )

    acc_ref[...] = jnp.zeros_like(acc_ref)
    att_ref[...] = jnp.zeros_like(att_ref)
    for place in range(PAIR):
        score(0, place)
        near_copy(place).wait()

    def one_pair(pair):
        later = jnp.minimum(pair + 1, pairs - 1)
        project(jnp.maximum(pair - 1, 0))
        for place in range(PAIR):
            slot = pair * PAIR + place
            att_ref[:, place * HD : (place + 1) * HD] = attended(
                score_ref[place], bias_ref[...], FAR_SLOTS + slot, kv_refs, order_ref
            )
            score(later, place)

        @pl.when(pair + 1 < pairs)
        def _():
            for place in range(PAIR):
                near_copy((pair + 1) * PAIR + place).wait()

    pl.loop(0, pairs)(one_pair)
    project(pairs - 1)
    pl.loop(0, FAR_SLOTS)(lambda slot: far_copy(slot).wait())


def last_kernel(nz, *refs):
    att_refs, (w_ref, acc_ref, out_ref, att_ref) = refs[:nz], refs[nz:]
    for slot in range(FAR_SLOTS):
        att_ref[:, slot * HD : (slot + 1) * HD] = jnp.concatenate([ref[slot] for ref in att_refs], axis=0)
    rows = att_refs[0].shape[1]
    z_at = lax.axis_index("kvring")
    for at in range(0, acc_ref.shape[1], TILE):
        mixed = acc_ref[:, at : at + TILE] + jnp.dot(
            att_ref[...], w_ref[:, at : at + TILE], preferred_element_type=jnp.float32
        )
        mixed = mixed.astype(jnp.bfloat16)
        for slot in range(nz):
            place = pl.multiple_of((z_at ^ partner_of(slot, nz)) * rows, rows)
            out_ref[pl.ds(place, rows), at : at + TILE] = mixed[slot * rows : (slot + 1) * rows]


def per_device_small_ring(queries, keys, values, doc_ids, head_mask, w_out):
    rows = queries.shape[0]
    nq = lax.axis_size("qring")
    nz = lax.axis_size("kvring")
    heads = head_mask.shape[0]
    width = w_out.shape[1]
    quarter = rows * nz
    total = quarter * nq
    rest_slots = heads - FAR_SLOTS - NEAR_SLOTS
    smem = pl.BlockSpec(memory_space=pltpu.SMEM)
    vmem = pl.BlockSpec(memory_space=pltpu.VMEM)
    hbm = pl.BlockSpec(memory_space=pl.ANY)
    params = pltpu.CompilerParams(vmem_limit_bytes=VMEM_LIMIT)

    def cost(micros):
        return pl.CostEstimate(flops=int(micros * 1e9), bytes_accessed=0, transcendentals=0)

    def slots_in_vmem(slots):
        return pltpu.VMEM((slots, rows, HD), jnp.bfloat16)

    kv_own = pl.pallas_call(
        join_kernel,
        out_shape=pltpu.VMEM((rows, 2 * keys.shape[1]), jnp.bfloat16),
        in_specs=[vmem, vmem],
        out_specs=vmem,
        name="join",
    )(keys, values)
    kv_parts = [kv_own, *swaps_along(kv_own, "kvring")]
    order, far, near, rest, bias = pl.pallas_call(
        functools.partial(prep_kernel, rows, nq, nz),
        out_shape=(
            pltpu.SMEM((heads + 1,), jnp.int32),
            *(slots_in_vmem(slots) for slots in (FAR_SLOTS, NEAR_SLOTS, rest_slots)),
            pltpu.VMEM((quarter, total), jnp.float32),
        ),
        in_specs=[smem, vmem, vmem],
        out_specs=[smem] + [vmem] * 4,
        cost_estimate=cost(4),
        name="prep",
    )(head_mask, doc_ids, queries)
    many = jnp.sum(head_mask) > NEAR_SLOTS + FAR_SLOTS
    *kv_parts, near, order, many = lax.optimization_barrier((*kv_parts, near, order, many))
    kv0 = jnp.concatenate(kv_parts, axis=0)
    kv2 = swap_along(kv0, "qring", 2)
    near_parts = [near, *swaps_along(near, "kvring")]
    rest_all = lax.cond(
        many,
        lambda array: jnp.concatenate([array, *swaps_along(array, "kvring")]),
        lambda array: jnp.zeros((nz * rest_slots, rows, HD), array.dtype),
        lax.optimization_barrier((rest, kv0))[0],
    )
    early = [near_parts[slot] for slot in EARLY]
    *early, kv2, rest_all = lax.optimization_barrier((*early, kv2, rest_all))
    for slot, part in zip(EARLY, early):
        near_parts[slot] = part
    kv02 = jnp.concatenate([kv0, kv2], axis=0)
    kv = (kv02, swap_along(kv02, "qring", 1))
    far_own = pl.pallas_call(
        functools.partial(own_kernel, len(kv)),
        out_shape=slots_in_vmem(FAR_SLOTS),
        in_specs=[smem] + [vmem] * (len(kv) + 2),
        out_specs=vmem,
        compiler_params=params,
        cost_estimate=cost(2),
        name="own",
    )(order, *in_vmem(*kv, far, bias))
    far_parts = [far_own, *swaps_along(far_own, "kvring")]
    acc, w_far = pl.pallas_call(
        functools.partial(first_kernel, len(kv), nz),
        out_shape=(
            pltpu.VMEM((quarter, width), jnp.float32),
            pltpu.VMEM((FAR_SLOTS * HD, width), jnp.bfloat16),
        ),
        in_specs=[smem] + [vmem] * (len(kv) + nz + 2) + [hbm],
        out_specs=(vmem, vmem),
        scratch_shapes=[
            pltpu.VMEM(((heads - FAR_SLOTS) * HD, width), jnp.bfloat16),
            pltpu.VMEM((heads - FAR_SLOTS, quarter, HD), jnp.bfloat16),
            pltpu.VMEM((quarter, PAIR * HD), jnp.bfloat16),
            pltpu.VMEM((PAIR, quarter, total), jnp.float32),
            pltpu.SemaphoreType.DMA((heads,)),
        ],
        compiler_params=params,
        cost_estimate=cost(6),
        name="first",
    )(order, *in_vmem(*kv, *near_parts, rest_all, bias), w_out)
    return pl.pallas_call(
        functools.partial(last_kernel, nz),
        out_shape=jax.ShapeDtypeStruct((quarter, width), jnp.bfloat16),
        in_specs=[vmem] * (nz + 2),
        out_specs=vmem,
        scratch_shapes=[pltpu.VMEM((quarter, FAR_SLOTS * HD), jnp.bfloat16)],
        compiler_params=params,
        name="last",
    )(*in_vmem(*far_parts, w_far, acc))


def solution(mesh):
    placed = (
        P(("groups", "qring", "kvring"), "head"),
        P(("groups", "qring", "kvring"), "head"),
        P(("groups", "qring", "kvring"), "head"),
        P("groups"),
        P("head"),
        P("head", "kvring"),
    )
    per_device = per_device_small_ring if small_ring(mesh) else per_device_any_ring
    return jax.shard_map(
        per_device,
        mesh=mesh,
        in_specs=placed,
        out_specs=P(("groups", "qring", "head"), "kvring"),
        check_vma=False,
    )
```

```python
import functools
import math

import jax
import jax.numpy as jnp
from jax import lax
from jax.experimental import pallas as pl
from jax.experimental.pallas import tpu as pltpu
from jax.sharding import PartitionSpec as P

HD = 128


NEG = -1e30


def block_rows(total_rows, shard_rows):
    best_size = shard_rows
    for multiple in range(1, total_rows // shard_rows + 1):
        if total_rows // shard_rows % multiple == 0 and multiple * shard_rows <= 256:
            best_size = multiple * shard_rows
    return best_size


def attend_keys(state, visible, queries4, key_rows, value_rows, scale_factor):
    run_max, run_sum, run_out = state
    mask4 = visible[:, None, None, :]
    scores = (
        jnp.einsum("rgec,kgc->rgek", queries4, key_rows, preferred_element_type=jnp.float32)
        * scale_factor
    )
    scores = jnp.where(mask4, scores, NEG)
    new_max = jnp.maximum(run_max, jnp.max(scores, axis=-1))
    weights = jnp.where(mask4, jnp.exp(scores - new_max[..., None]), 0.0)
    shrink = jnp.exp(run_max - new_max)
    run_sum = run_sum * shrink + jnp.sum(weights, axis=-1)
    update = jnp.einsum(
        "rgek,kgc->rgec",
        weights.astype(jnp.bfloat16),
        value_rows,
        preferred_element_type=jnp.float32,
    )
    run_out = run_out * shrink[..., None] + update
    return (new_max, run_sum, run_out)


def fold_piece(
    state, pieces, key_start, queries4, query_doc, query_pos, doc_ids, shard_rows, scale_factor
):
    key_all, value_all = pieces
    total_rows = key_all.shape[0]
    block_size = block_rows(total_rows, shard_rows)

    def one_block(index, carry):
        offset = index * block_size
        key_rows = lax.dynamic_slice_in_dim(key_all, offset, block_size, 0)
        value_rows = lax.dynamic_slice_in_dim(value_all, offset, block_size, 0)
        first = key_start + offset
        key_doc = lax.dynamic_slice_in_dim(doc_ids, first, block_size, 0)
        key_pos = first + jnp.arange(block_size, dtype=jnp.int32)
        visible = (query_doc[:, None] == key_doc[None, :]) & (
            key_pos[None, :] <= query_pos[:, None]
        )
        return attend_keys(carry, visible, queries4, key_rows, value_rows, scale_factor)

    return lax.fori_loop(0, total_rows // block_size, one_block, state)


def per_device_any_ring(queries, keys, values, doc_ids, head_mask, w_out):
    shard_rows = queries.shape[0]
    kv_local = keys.shape[1] // HD
    q_local = queries.shape[1] // HD
    per_group = q_local // kv_local
    scale_factor = 1.0 / math.sqrt(HD)
    cycle_size = lax.axis_size("kvring")
    cycle_index = lax.axis_index("kvring")
    loop_index = lax.axis_index("qring")
    quarter = cycle_size * shard_rows
    key_rows = keys.reshape(shard_rows, kv_local, HD)
    value_rows = values.reshape(shard_rows, kv_local, HD)
    loop_size = lax.axis_size("qring")
    gathered = lax.all_gather(queries, "qring", axis=0, tiled=True)
    query_total = loop_size * shard_rows
    row_ids = jnp.arange(query_total, dtype=jnp.int32)
    query_pos = row_ids // shard_rows * quarter + cycle_index * shard_rows + row_ids % shard_rows
    queries4 = gathered.reshape(query_total, kv_local, per_group, HD)
    query_doc = jnp.take(doc_ids, query_pos)
    key_base = loop_index * quarter
    initial = (
        jnp.full((query_total, kv_local, per_group), NEG, jnp.float32),
        jnp.zeros((query_total, kv_local, per_group), jnp.float32),
        jnp.zeros((query_total, kv_local, per_group, HD), jnp.float32),
    )
    run_max, run_sum, run_out = fold_piece(
        initial,
        (
            lax.all_gather(key_rows, "kvring", axis=0, tiled=True),
            lax.all_gather(value_rows, "kvring", axis=0, tiled=True),
        ),
        key_base,
        queries4,
        query_doc,
        query_pos,
        doc_ids,
        shard_rows,
        scale_factor,
    )
    top = lax.pmax(run_max, "qring")
    factor = jnp.exp(run_max - top)
    numer, denom = (
        lax.psum_scatter(
            (run_out * factor[..., None]).astype(jnp.bfloat16),
            "qring",
            scatter_dimension=0,
            tiled=True,
        ).astype(jnp.float32),
        lax.psum_scatter(
            (run_sum * factor).astype(jnp.bfloat16), "qring", scatter_dimension=0, tiled=True
        ).astype(jnp.float32),
    )
    mask_f = head_mask.reshape(kv_local, per_group).astype(jnp.float32)
    attended = (
        (numer / denom[..., None] * mask_f[None, :, :, None])
        .astype(jnp.bfloat16)
        .reshape(shard_rows, q_local * HD)
    )
    partial_sum = jnp.dot(
        lax.all_gather(attended, "kvring", axis=0, tiled=True),
        w_out,
        preferred_element_type=jnp.float32,
    )
    return lax.psum_scatter(
        partial_sum.astype(jnp.bfloat16), "head", scatter_dimension=0, tiled=True
    )


VMEM_LIMIT = 24 * 1024 * 1024
LOG2E = math.log2(math.e)
PAIR = 2
NEAR_SLOTS = 16
EARLY_PARTS = 2
EARLY_COST = 0
FIRST_COST = 6
FAR_SLOTS = 10
TILE = 1024


def small_ring(mesh):
    return (mesh.shape["qring"], mesh.shape["kvring"], mesh.shape["head"]) == (4, 4, 1)


def swap_along(array, axis_name, partner):
    size = lax.axis_size(axis_name)
    return lax.ppermute(array, axis_name, [(i, i ^ partner) for i in range(size)])


def partner_of(slot, count):
    return (count - slot) % count


def swaps_along(array, axis_name):
    size = lax.axis_size(axis_name)
    return [swap_along(array, axis_name, partner_of(slot, size)) for slot in range(1, size)]


def in_vmem(*arrays):
    return [pltpu.with_memory_space_constraint(array, pltpu.VMEM) for array in arrays]


def slot_of(index, width, count):
    slot = jnp.zeros_like(index)
    for bound in range(1, count):
        slot = slot + (index >= bound * width).astype(jnp.int32)
    return slot


def rows_of(slot):
    return pl.ds(pl.multiple_of(slot * HD, HD), HD)


def join_kernel(k_ref, v_ref, out_ref):
    width = k_ref.shape[1]
    out_ref[:, :width] = k_ref[...]
    out_ref[:, width:] = v_ref[...]


def prep_kernel(rows, nq, nz, mask_ref, doc_ref, q_ref, order_ref, *refs):
    *slot_refs, bias_ref = refs
    heads = mask_ref.shape[0]
    for slot in range(heads):
        order_ref[slot] = 0
    kept = jnp.int32(0)
    for head in range(heads):
        order_ref[kept] = head
        kept = kept + mask_ref[head]
    order_ref[heads] = kept
    slot = 0
    for ref in slot_refs:
        for place in range(ref.shape[0]):
            ref[place] = q_ref[:, rows_of(order_ref[slot])]
            slot += 1
    quarter = rows * nz
    total = quarter * nq
    q_at = lax.axis_index("qring")
    z_at = lax.axis_index("kvring")
    doc = doc_ref[...].reshape(1, total)
    row = lax.broadcasted_iota(jnp.int32, (quarter, 1), 0)
    row_z = slot_of(row, rows, nz)
    row_pos = q_at * quarter + (partner_of(row_z, nz) ^ z_at) * rows + row - row_z * rows
    col = lax.broadcasted_iota(jnp.int32, (1, total), 1)
    col_q = slot_of(col, quarter, nq)
    rest = col - col_q * quarter
    col_z = slot_of(rest, rows, nz)
    col_pos = (((col_q & 1) * 2 + (col_q >> 1)) ^ q_at) * quarter + (partner_of(col_z, nz) ^ z_at) * rows + rest - col_z * rows
    own_doc = jnp.sum(jnp.where(col == row_pos, doc, 0), axis=1, keepdims=True)
    first = jnp.sum((doc < own_doc).astype(jnp.int32), axis=1, keepdims=True)
    bias_ref[...] = jnp.where((col_pos >= first) & (col_pos <= row_pos), 0.0, NEG)


def kv_at(slot, kv_refs, order_ref, is_value):
    heads = order_ref.shape[0] - 1
    kv_heads = kv_refs[0].shape[1] // (2 * HD)
    group = order_ref[slot] // (heads // kv_heads) + is_value * kv_heads
    return jnp.concatenate([ref[:, rows_of(group)] for ref in kv_refs], axis=0)


def scores_of(q, slot, kv_refs, order_ref):
    k = kv_at(slot, kv_refs, order_ref, 0)
    return lax.dot_general(q, k, (((1,), (1,)), ((), ())), preferred_element_type=jnp.float32)


def attended(scores, bias, slot, kv_refs, order_ref):
    scores = scores * (LOG2E / math.sqrt(HD)) + bias
    weights = jnp.exp2(scores - jnp.max(scores, axis=1, keepdims=True))
    v = kv_at(slot, kv_refs, order_ref, 1)
    v_and_ones = jnp.concatenate([v, jnp.ones_like(v)], axis=1)
    sums = jnp.dot(weights.astype(jnp.bfloat16), v_and_ones, preferred_element_type=jnp.float32)
    keep = (slot < order_ref[order_ref.shape[0] - 1]).astype(jnp.float32)
    return (sums[:, :HD] * (keep / sums[:, HD:])).astype(jnp.bfloat16)


def own_kernel(kvs, order_ref, *refs):
    kv_refs, (q_ref, bias_ref, att_ref) = refs[:kvs], refs[kvs:]
    rows = q_ref.shape[1]

    def one_slot(slot):
        scores = scores_of(q_ref[slot], slot, kv_refs, order_ref)
        att_ref[slot] = attended(scores, bias_ref[:rows], slot, kv_refs, order_ref)

    pl.loop(0, FAR_SLOTS, unroll=FAR_SLOTS // 2)(one_slot)


def pairs_of(order_ref):
    heads = order_ref.shape[0] - 1
    rest_slots = heads - FAR_SLOTS - NEAR_SLOTS
    extra = jnp.clip((order_ref[heads] - FAR_SLOTS - NEAR_SLOTS + PAIR - 1) // PAIR, 0, rest_slots // PAIR)
    return NEAR_SLOTS // PAIR + extra, extra


def place_queries(parts, extra, near_refs, rest_ref, q_ref):
    rest_slots = q_ref.shape[0] - NEAR_SLOTS
    for slot in range(NEAR_SLOTS):
        q_ref[slot] = jnp.concatenate([ref[slot] for ref in near_refs], axis=0)

    @pl.when(extra > 0)
    def _():
        for slot in range(rest_slots):
            rows = [rest_ref[part * rest_slots + slot] for part in parts]
            q_ref[NEAR_SLOTS + slot] = jnp.concatenate(rows, axis=0)


def attend_pairs(pairs, q_ref, score_ref, bias, kv_refs, order_ref, keep, between):
    def score(pair, place):
        slot = pair * PAIR + place
        score_ref[place] = scores_of(q_ref[slot], FAR_SLOTS + slot, kv_refs, order_ref)

    for place in range(PAIR):
        score(0, place)

    def one_pair(pair):
        later = jnp.minimum(pair + 1, pairs - 1)
        between(pair)
        for place in range(PAIR):
            slot = pair * PAIR + place
            keep(slot, place, attended(score_ref[place], bias, FAR_SLOTS + slot, kv_refs, order_ref))
            score(later, place)

    pl.loop(0, pairs)(one_pair)


def w_copy(order_ref, w_hbm, w_ref, sem, start, slot):
    return pltpu.make_async_copy(w_hbm.at[rows_of(order_ref[start + slot])], w_ref.at[rows_of(slot)], sem.at[slot])


def early_kernel(kvs, order_ref, *refs):
    kv_refs, near_refs = refs[:kvs], refs[kvs : kvs + EARLY_PARTS]
    rest_ref, bias_ref, w_hbm, early_ref, w_ref, q_ref, score_ref, sem = refs[kvs + EARLY_PARTS :]
    pairs, extra = pairs_of(order_ref)
    copy_of = functools.partial(w_copy, order_ref, w_hbm, w_ref, sem, FAR_SLOTS)
    pl.loop(0, pairs * PAIR)(lambda slot: copy_of(slot).start())
    place_queries(range(EARLY_PARTS), extra, near_refs, rest_ref, q_ref)
    rows = q_ref.shape[1]

    def keep(slot, place, rows_attended):
        early_ref[slot] = rows_attended

    attend_pairs(pairs, q_ref, score_ref, bias_ref[:rows], kv_refs, order_ref, keep, lambda pair: None)
    pl.loop(0, pairs * PAIR)(lambda slot: copy_of(slot).wait())


def first_kernel(kvs, nz, order_ref, *refs):
    late = nz - EARLY_PARTS
    kv_refs, near_refs = refs[:kvs], refs[kvs : kvs + late]
    rest_ref, early_ref, bias_ref, w_ref, w_hbm, acc_ref, w_far_ref, q_ref, att_ref, score_ref, sem = refs[kvs + late :]
    pairs, extra = pairs_of(order_ref)
    copy_of = functools.partial(w_copy, order_ref, w_hbm, w_far_ref, sem, 0)
    pl.loop(0, FAR_SLOTS)(lambda slot: copy_of(slot).start())

    place_queries(range(EARLY_PARTS, nz), extra, near_refs, rest_ref, q_ref)
    done = early_ref.shape[1]

    def project(pair):
        rows = pl.ds(pl.multiple_of(pair * PAIR * HD, HD), PAIR * HD)
        for at in range(0, acc_ref.shape[1], TILE):
            acc_ref[:, at : at + TILE] += jnp.dot(
                att_ref[...], w_ref[rows, at : at + TILE], preferred_element_type=jnp.float32
            )

    def keep(slot, place, rows_attended):
        att_ref[:done, place * HD : (place + 1) * HD] = early_ref[slot]
        att_ref[done:, place * HD : (place + 1) * HD] = rows_attended

    def between(pair):
        project(jnp.maximum(pair - 1, 0))

    acc_ref[...] = jnp.zeros_like(acc_ref)
    att_ref[...] = jnp.zeros_like(att_ref)
    attend_pairs(pairs, q_ref, score_ref, bias_ref[done:], kv_refs, order_ref, keep, between)
    project(pairs - 1)
    pl.loop(0, FAR_SLOTS)(lambda slot: copy_of(slot).wait())


def last_kernel(nz, *refs):
    att_refs, (w_ref, acc_ref, out_ref, att_ref) = refs[:nz][::-1], refs[nz:]
    for slot in range(FAR_SLOTS):
        att_ref[:, slot * HD : (slot + 1) * HD] = jnp.concatenate([ref[slot] for ref in att_refs], axis=0)
    rows = att_refs[0].shape[1]
    z_at = lax.axis_index("kvring")
    for at in range(0, acc_ref.shape[1], TILE):
        mixed = acc_ref[:, at : at + TILE] + jnp.dot(
            att_ref[...], w_ref[:, at : at + TILE], preferred_element_type=jnp.float32
        )
        mixed = mixed.astype(jnp.bfloat16)
        for slot in range(nz):
            place = pl.multiple_of((z_at ^ partner_of(slot, nz)) * rows, rows)
            out_ref[pl.ds(place, rows), at : at + TILE] = mixed[slot * rows : (slot + 1) * rows]


def per_device_small_ring(queries, keys, values, doc_ids, head_mask, w_out):
    rows = queries.shape[0]
    nq = lax.axis_size("qring")
    nz = lax.axis_size("kvring")
    heads = head_mask.shape[0]
    width = w_out.shape[1]
    quarter = rows * nz
    total = quarter * nq
    rest_slots = heads - FAR_SLOTS - NEAR_SLOTS
    smem = pl.BlockSpec(memory_space=pltpu.SMEM)
    vmem = pl.BlockSpec(memory_space=pltpu.VMEM)
    hbm = pl.BlockSpec(memory_space=pltpu.HBM)
    params = pltpu.CompilerParams(vmem_limit_bytes=VMEM_LIMIT)

    def cost(micros):
        return pl.CostEstimate(flops=int(micros * 1e9), bytes_accessed=0, transcendentals=0)

    def slots_in_vmem(slots):
        return pltpu.VMEM((slots, rows, HD), jnp.bfloat16)

    kv_own = pl.pallas_call(
        join_kernel,
        out_shape=pltpu.VMEM((rows, 2 * keys.shape[1]), jnp.bfloat16),
        in_specs=[vmem, vmem],
        out_specs=vmem,
        name="join",
    )(keys, values)
    kv_parts = [kv_own, *swaps_along(kv_own, "kvring")]
    order, far, near, rest, bias = pl.pallas_call(
        functools.partial(prep_kernel, rows, nq, nz),
        out_shape=(
            pltpu.SMEM((heads + 1,), jnp.int32),
            *(slots_in_vmem(slots) for slots in (FAR_SLOTS, NEAR_SLOTS, rest_slots)),
            pltpu.VMEM((quarter, total), jnp.float32),
        ),
        in_specs=[smem, vmem, vmem],
        out_specs=[smem] + [vmem] * 4,
        cost_estimate=cost(4),
        name="prep",
    )(head_mask, doc_ids, queries)
    many = jnp.sum(head_mask) > NEAR_SLOTS + FAR_SLOTS
    *kv_parts, near, order, many = lax.optimization_barrier((*kv_parts, near, order, many))
    kv0 = jnp.concatenate(kv_parts, axis=0)
    kv2 = swap_along(kv0, "qring", 2)
    near_parts = [near, *swaps_along(near, "kvring")]
    rest_all = lax.cond(
        many,
        lambda array: jnp.concatenate([array, *swaps_along(array, "kvring")]),
        lambda array: jnp.zeros((nz * rest_slots, rows, HD), array.dtype),
        lax.optimization_barrier((rest, kv0))[0],
    )
    near_parts[1], kv2, rest_all = lax.optimization_barrier((near_parts[1], kv2, rest_all))
    kv02 = jnp.concatenate([kv0, kv2], axis=0)
    kv = (kv02, swap_along(kv02, "qring", 1))
    far_own = pl.pallas_call(
        functools.partial(own_kernel, len(kv)),
        out_shape=slots_in_vmem(FAR_SLOTS),
        in_specs=[smem] + [vmem] * (len(kv) + 2),
        out_specs=vmem,
        compiler_params=params,
        cost_estimate=cost(2),
        name="own",
    )(order, *in_vmem(*kv, far, bias))
    far_parts = [far_own, *swaps_along(far_own, "kvring")]
    near_slots = heads - FAR_SLOTS
    early_rows = EARLY_PARTS * rows
    late_rows = quarter - early_rows
    order_early = lax.optimization_barrier((order, far_own))[0]
    hbm = pl.BlockSpec(memory_space=pltpu.HBM)
    early, w_near = pl.pallas_call(
        functools.partial(early_kernel, len(kv)),
        out_shape=(
            pltpu.VMEM((near_slots, early_rows, HD), jnp.bfloat16),
            pltpu.VMEM((near_slots * HD, width), jnp.bfloat16),
        ),
        in_specs=[smem] + [vmem] * (len(kv) + EARLY_PARTS + 2) + [hbm],
        out_specs=(vmem, vmem),
        scratch_shapes=[
            pltpu.VMEM((near_slots, early_rows, HD), jnp.bfloat16),
            pltpu.VMEM((PAIR, early_rows, total), jnp.float32),
            pltpu.SemaphoreType.DMA((near_slots,)),
        ],
        compiler_params=params,
        cost_estimate=cost(EARLY_COST),
        name="early",
    )(order_early, *in_vmem(*kv, *near_parts[:EARLY_PARTS], rest_all, bias), w_out)
    acc, w_far = pl.pallas_call(
        functools.partial(first_kernel, len(kv), nz),
        out_shape=(
            pltpu.VMEM((quarter, width), jnp.float32),
            pltpu.VMEM((FAR_SLOTS * HD, width), jnp.bfloat16),
        ),
        in_specs=[smem] + [vmem] * (len(kv) + nz - EARLY_PARTS + 4) + [hbm],
        out_specs=(vmem, vmem),
        scratch_shapes=[
            pltpu.VMEM((near_slots, late_rows, HD), jnp.bfloat16),
            pltpu.VMEM((quarter, PAIR * HD), jnp.bfloat16),
            pltpu.VMEM((PAIR, late_rows, total), jnp.float32),
            pltpu.SemaphoreType.DMA((FAR_SLOTS,)),
        ],
        compiler_params=params,
        cost_estimate=cost(FIRST_COST),
        name="first",
    )(order, *in_vmem(*kv, *near_parts[EARLY_PARTS:], rest_all, early, bias, w_near), w_out)
    return pl.pallas_call(
        functools.partial(last_kernel, nz),
        out_shape=jax.ShapeDtypeStruct((quarter, width), jnp.bfloat16),
        in_specs=[vmem] * (nz + 2),
        out_specs=vmem,
        scratch_shapes=[pltpu.VMEM((quarter, FAR_SLOTS * HD), jnp.bfloat16)],
        compiler_params=params,
        name="last",
    )(*in_vmem(*far_parts[::-1], w_far, acc))


def solution(mesh):
    placed = (
        P(("groups", "qring", "kvring"), "head"),
        P(("groups", "qring", "kvring"), "head"),
        P(("groups", "qring", "kvring"), "head"),
        P("groups"),
        P("head"),
        P("head", "kvring"),
    )
    per_device = per_device_small_ring if small_ring(mesh) else per_device_any_ring
    return jax.shard_map(
        per_device,
        mesh=mesh,
        in_specs=placed,
        out_specs=P(("groups", "qring", "head"), "kvring"),
        check_vma=False,
    )
```

```python
import functools
import math

import jax
import jax.numpy as jnp
from jax import lax
from jax.experimental import pallas as pl
from jax.experimental.pallas import tpu as pltpu
from jax.sharding import PartitionSpec as P

HD = 128


NEG = -1e30


def block_rows(total_rows, shard_rows):
    best_size = shard_rows
    for multiple in range(1, total_rows // shard_rows + 1):
        if total_rows // shard_rows % multiple == 0 and multiple * shard_rows <= 256:
            best_size = multiple * shard_rows
    return best_size


def attend_keys(state, visible, queries4, key_rows, value_rows, scale_factor):
    run_max, run_sum, run_out = state
    mask4 = visible[:, None, None, :]
    scores = (
        jnp.einsum("rgec,kgc->rgek", queries4, key_rows, preferred_element_type=jnp.float32)
        * scale_factor
    )
    scores = jnp.where(mask4, scores, NEG)
    new_max = jnp.maximum(run_max, jnp.max(scores, axis=-1))
    weights = jnp.where(mask4, jnp.exp(scores - new_max[..., None]), 0.0)
    shrink = jnp.exp(run_max - new_max)
    run_sum = run_sum * shrink + jnp.sum(weights, axis=-1)
    update = jnp.einsum(
        "rgek,kgc->rgec",
        weights.astype(jnp.bfloat16),
        value_rows,
        preferred_element_type=jnp.float32,
    )
    run_out = run_out * shrink[..., None] + update
    return (new_max, run_sum, run_out)


def fold_piece(
    state, pieces, key_start, queries4, query_doc, query_pos, doc_ids, shard_rows, scale_factor
):
    key_all, value_all = pieces
    total_rows = key_all.shape[0]
    block_size = block_rows(total_rows, shard_rows)

    def one_block(index, carry):
        offset = index * block_size
        key_rows = lax.dynamic_slice_in_dim(key_all, offset, block_size, 0)
        value_rows = lax.dynamic_slice_in_dim(value_all, offset, block_size, 0)
        first = key_start + offset
        key_doc = lax.dynamic_slice_in_dim(doc_ids, first, block_size, 0)
        key_pos = first + jnp.arange(block_size, dtype=jnp.int32)
        visible = (query_doc[:, None] == key_doc[None, :]) & (
            key_pos[None, :] <= query_pos[:, None]
        )
        return attend_keys(carry, visible, queries4, key_rows, value_rows, scale_factor)

    return lax.fori_loop(0, total_rows // block_size, one_block, state)


def per_device_any_ring(queries, keys, values, doc_ids, head_mask, w_out):
    shard_rows = queries.shape[0]
    kv_local = keys.shape[1] // HD
    q_local = queries.shape[1] // HD
    per_group = q_local // kv_local
    scale_factor = 1.0 / math.sqrt(HD)
    cycle_size = lax.axis_size("kvring")
    cycle_index = lax.axis_index("kvring")
    loop_index = lax.axis_index("qring")
    quarter = cycle_size * shard_rows
    key_rows = keys.reshape(shard_rows, kv_local, HD)
    value_rows = values.reshape(shard_rows, kv_local, HD)
    loop_size = lax.axis_size("qring")
    gathered = lax.all_gather(queries, "qring", axis=0, tiled=True)
    query_total = loop_size * shard_rows
    row_ids = jnp.arange(query_total, dtype=jnp.int32)
    query_pos = row_ids // shard_rows * quarter + cycle_index * shard_rows + row_ids % shard_rows
    queries4 = gathered.reshape(query_total, kv_local, per_group, HD)
    query_doc = jnp.take(doc_ids, query_pos)
    key_base = loop_index * quarter
    initial = (
        jnp.full((query_total, kv_local, per_group), NEG, jnp.float32),
        jnp.zeros((query_total, kv_local, per_group), jnp.float32),
        jnp.zeros((query_total, kv_local, per_group, HD), jnp.float32),
    )
    run_max, run_sum, run_out = fold_piece(
        initial,
        (
            lax.all_gather(key_rows, "kvring", axis=0, tiled=True),
            lax.all_gather(value_rows, "kvring", axis=0, tiled=True),
        ),
        key_base,
        queries4,
        query_doc,
        query_pos,
        doc_ids,
        shard_rows,
        scale_factor,
    )
    top = lax.pmax(run_max, "qring")
    factor = jnp.exp(run_max - top)
    numer, denom = (
        lax.psum_scatter(
            (run_out * factor[..., None]).astype(jnp.bfloat16),
            "qring",
            scatter_dimension=0,
            tiled=True,
        ).astype(jnp.float32),
        lax.psum_scatter(
            (run_sum * factor).astype(jnp.bfloat16), "qring", scatter_dimension=0, tiled=True
        ).astype(jnp.float32),
    )
    mask_f = head_mask.reshape(kv_local, per_group).astype(jnp.float32)
    attended = (
        (numer / denom[..., None] * mask_f[None, :, :, None])
        .astype(jnp.bfloat16)
        .reshape(shard_rows, q_local * HD)
    )
    partial_sum = jnp.dot(
        lax.all_gather(attended, "kvring", axis=0, tiled=True),
        w_out,
        preferred_element_type=jnp.float32,
    )
    return lax.psum_scatter(
        partial_sum.astype(jnp.bfloat16), "head", scatter_dimension=0, tiled=True
    )


VMEM_LIMIT = 24 * 1024 * 1024
LOG2E = math.log2(math.e)
PAIR = 2
NEAR_SLOTS = 16
EARLY_PARTS = 2
EARLY_COST = 0
FIRST_COST = 6
FAR_SLOTS = 10
TILE = 1024
LAST_TILE = 512


def small_ring(mesh):
    return (mesh.shape["qring"], mesh.shape["kvring"], mesh.shape["head"]) == (4, 4, 1)


def swap_along(array, axis_name, partner):
    size = lax.axis_size(axis_name)
    return lax.ppermute(array, axis_name, [(i, i ^ partner) for i in range(size)])


def partner_of(slot, count):
    return (count - slot) % count


def swaps_along(array, axis_name):
    size = lax.axis_size(axis_name)
    return [swap_along(array, axis_name, partner_of(slot, size)) for slot in range(1, size)]


def in_vmem(*arrays):
    return [pltpu.with_memory_space_constraint(array, pltpu.VMEM) for array in arrays]


def slot_of(index, width, count):
    slot = jnp.zeros_like(index)
    for bound in range(1, count):
        slot = slot + (index >= bound * width).astype(jnp.int32)
    return slot


def rows_of(slot):
    return pl.ds(pl.multiple_of(slot * HD, HD), HD)


def join_kernel(k_ref, v_ref, out_ref):
    width = k_ref.shape[1]
    out_ref[:, :width] = k_ref[...]
    out_ref[:, width:] = v_ref[...]


def prep_kernel(rows, nq, nz, mask_ref, doc_ref, q_ref, order_ref, *refs):
    *slot_refs, bias_ref = refs
    heads = mask_ref.shape[0]
    for slot in range(heads):
        order_ref[slot] = 0
    kept = jnp.int32(0)
    for head in range(heads):
        order_ref[kept] = head
        kept = kept + mask_ref[head]
    order_ref[heads] = kept
    slot = 0
    for ref in slot_refs:
        for place in range(ref.shape[0]):
            ref[place] = q_ref[:, rows_of(order_ref[slot])]
            slot += 1
    quarter = rows * nz
    total = quarter * nq
    q_at = lax.axis_index("qring")
    z_at = lax.axis_index("kvring")
    doc = doc_ref[...].reshape(1, total)
    row = lax.broadcasted_iota(jnp.int32, (quarter, 1), 0)
    row_z = slot_of(row, rows, nz)
    row_pos = q_at * quarter + (partner_of(row_z, nz) ^ z_at) * rows + row - row_z * rows
    col = lax.broadcasted_iota(jnp.int32, (1, total), 1)
    col_q = slot_of(col, quarter, nq)
    rest = col - col_q * quarter
    col_z = slot_of(rest, rows, nz)
    col_pos = (((col_q & 1) * 2 + (col_q >> 1)) ^ q_at) * quarter + (partner_of(col_z, nz) ^ z_at) * rows + rest - col_z * rows
    own_doc = jnp.sum(jnp.where(col == row_pos, doc, 0), axis=1, keepdims=True)
    first = jnp.sum((doc < own_doc).astype(jnp.int32), axis=1, keepdims=True)
    bias_ref[...] = jnp.where((col_pos >= first) & (col_pos <= row_pos), 0.0, NEG)


def kv_at(slot, kv_refs, order_ref, is_value):
    heads = order_ref.shape[0] - 1
    kv_heads = kv_refs[0].shape[1] // (2 * HD)
    group = order_ref[slot] // (heads // kv_heads) + is_value * kv_heads
    return jnp.concatenate([ref[:, rows_of(group)] for ref in kv_refs], axis=0)


def scores_of(q, slot, kv_refs, order_ref):
    k = kv_at(slot, kv_refs, order_ref, 0)
    return lax.dot_general(q, k, (((1,), (1,)), ((), ())), preferred_element_type=jnp.float32)


def attended(scores, bias, slot, kv_refs, order_ref):
    scores = scores * (LOG2E / math.sqrt(HD)) + bias
    weights = jnp.exp2(scores - jnp.max(scores, axis=1, keepdims=True))
    v = kv_at(slot, kv_refs, order_ref, 1)
    v_and_ones = jnp.concatenate([v, jnp.ones_like(v)], axis=1)
    sums = jnp.dot(weights.astype(jnp.bfloat16), v_and_ones, preferred_element_type=jnp.float32)
    keep = (slot < order_ref[order_ref.shape[0] - 1]).astype(jnp.float32)
    return (sums[:, :HD] * (keep / sums[:, HD:])).astype(jnp.bfloat16)


def own_kernel(kvs, order_ref, *refs):
    kv_refs, (q_ref, bias_ref, att_ref) = refs[:kvs], refs[kvs:]
    rows = q_ref.shape[1]

    def one_slot(slot):
        scores = scores_of(q_ref[slot], slot, kv_refs, order_ref)
        att_ref[slot] = attended(scores, bias_ref[:rows], slot, kv_refs, order_ref)

    pl.loop(0, FAR_SLOTS, unroll=FAR_SLOTS // 2)(one_slot)


def pairs_of(order_ref):
    heads = order_ref.shape[0] - 1
    rest_slots = heads - FAR_SLOTS - NEAR_SLOTS
    extra = jnp.clip((order_ref[heads] - FAR_SLOTS - NEAR_SLOTS + PAIR - 1) // PAIR, 0, rest_slots // PAIR)
    return NEAR_SLOTS // PAIR + extra, extra


def place_queries(parts, extra, near_refs, rest_ref, q_ref):
    rest_slots = q_ref.shape[0] - NEAR_SLOTS
    for slot in range(NEAR_SLOTS):
        q_ref[slot] = jnp.concatenate([ref[slot] for ref in near_refs], axis=0)

    @pl.when(extra > 0)
    def _():
        for slot in range(rest_slots):
            rows = [rest_ref[part * rest_slots + slot] for part in parts]
            q_ref[NEAR_SLOTS + slot] = jnp.concatenate(rows, axis=0)


def attend_pairs(pairs, q_ref, score_ref, bias, kv_refs, order_ref, keep, between):
    def score(pair, place):
        slot = pair * PAIR + place
        score_ref[place] = scores_of(q_ref[slot], FAR_SLOTS + slot, kv_refs, order_ref)

    for place in range(PAIR):
        score(0, place)

    def one_pair(pair):
        later = jnp.minimum(pair + 1, pairs - 1)
        between(pair)
        for place in range(PAIR):
            slot = pair * PAIR + place
            keep(slot, place, attended(score_ref[place], bias, FAR_SLOTS + slot, kv_refs, order_ref))
            score(later, place)

    pl.loop(0, pairs)(one_pair)


def w_copy(order_ref, w_hbm, w_ref, sem, start, slot):
    return pltpu.make_async_copy(w_hbm.at[rows_of(order_ref[start + slot])], w_ref.at[rows_of(slot)], sem.at[slot])


def early_kernel(kvs, order_ref, *refs):
    kv_refs, near_refs = refs[:kvs], refs[kvs : kvs + EARLY_PARTS]
    rest_ref, bias_ref, w_hbm, early_ref, w_ref, q_ref, score_ref, sem = refs[kvs + EARLY_PARTS :]
    pairs, extra = pairs_of(order_ref)
    copy_of = functools.partial(w_copy, order_ref, w_hbm, w_ref, sem, FAR_SLOTS)
    pl.loop(0, pairs * PAIR)(lambda slot: copy_of(slot).start())
    place_queries(range(EARLY_PARTS), extra, near_refs, rest_ref, q_ref)
    rows = q_ref.shape[1]

    def keep(slot, place, rows_attended):
        early_ref[slot] = rows_attended

    attend_pairs(pairs, q_ref, score_ref, bias_ref[:rows], kv_refs, order_ref, keep, lambda pair: None)
    pl.loop(0, pairs * PAIR)(lambda slot: copy_of(slot).wait())


def first_kernel(kvs, nz, order_ref, *refs):
    late = nz - EARLY_PARTS
    kv_refs, near_refs = refs[:kvs], refs[kvs : kvs + late]
    rest_ref, early_ref, bias_ref, w_ref, w_hbm, acc_ref, w_far_ref, q_ref, att_ref, score_ref, sem = refs[kvs + late :]
    pairs, extra = pairs_of(order_ref)
    copy_of = functools.partial(w_copy, order_ref, w_hbm, w_far_ref, sem, 0)
    pl.loop(0, FAR_SLOTS)(lambda slot: copy_of(slot).start())

    place_queries(range(EARLY_PARTS, nz), extra, near_refs, rest_ref, q_ref)
    done = early_ref.shape[1]

    def project(pair):
        rows = pl.ds(pl.multiple_of(pair * PAIR * HD, HD), PAIR * HD)
        for at in range(0, acc_ref.shape[1], TILE):
            acc_ref[:, at : at + TILE] += jnp.dot(
                att_ref[...], w_ref[rows, at : at + TILE], preferred_element_type=jnp.float32
            )

    def keep(slot, place, rows_attended):
        att_ref[:done, place * HD : (place + 1) * HD] = early_ref[slot]
        att_ref[done:, place * HD : (place + 1) * HD] = rows_attended

    def between(pair):
        project(jnp.maximum(pair - 1, 0))

    acc_ref[...] = jnp.zeros_like(acc_ref)
    att_ref[...] = jnp.zeros_like(att_ref)
    attend_pairs(pairs, q_ref, score_ref, bias_ref[done:], kv_refs, order_ref, keep, between)
    project(pairs - 1)
    pl.loop(0, FAR_SLOTS)(lambda slot: copy_of(slot).wait())


def last_kernel(nz, *refs):
    *refs, out_hbm, att_ref, out_ref, sem = refs
    refs = [*refs, out_ref, att_ref]
    copies = []
    att_refs, (w_ref, acc_ref, out_ref, att_ref) = refs[:nz][::-1], refs[nz:]
    for slot in range(FAR_SLOTS):
        att_ref[:, slot * HD : (slot + 1) * HD] = jnp.concatenate([ref[slot] for ref in att_refs], axis=0)
    rows = att_refs[0].shape[1]
    z_at = lax.axis_index("kvring")
    for index, at in enumerate(range(0, acc_ref.shape[1], LAST_TILE)):
        tile = slice(at, at + LAST_TILE)
        mixed = acc_ref[:, tile] + jnp.dot(att_ref[...], w_ref[:, tile], preferred_element_type=jnp.float32)
        mixed = mixed.astype(jnp.bfloat16)
        for slot in range(nz):
            place = pl.multiple_of((z_at ^ partner_of(slot, nz)) * rows, rows)
            out_ref[pl.ds(place, rows), tile] = mixed[slot * rows : (slot + 1) * rows]
        copies.append(pltpu.make_async_copy(out_ref.at[:, tile], out_hbm.at[:, tile], sem.at[index]))
        copies[-1].start()
    for copy in copies:
        copy.wait()


def per_device_small_ring(queries, keys, values, doc_ids, head_mask, w_out):
    rows = queries.shape[0]
    nq = lax.axis_size("qring")
    nz = lax.axis_size("kvring")
    heads = head_mask.shape[0]
    width = w_out.shape[1]
    quarter = rows * nz
    total = quarter * nq
    rest_slots = heads - FAR_SLOTS - NEAR_SLOTS
    smem = pl.BlockSpec(memory_space=pltpu.SMEM)
    vmem = pl.BlockSpec(memory_space=pltpu.VMEM)
    hbm = pl.BlockSpec(memory_space=pltpu.HBM)
    params = pltpu.CompilerParams(vmem_limit_bytes=VMEM_LIMIT)

    def cost(micros):
        return pl.CostEstimate(flops=int(micros * 1e9), bytes_accessed=0, transcendentals=0)

    def slots_in_vmem(slots):
        return pltpu.VMEM((slots, rows, HD), jnp.bfloat16)

    kv_own = pl.pallas_call(
        join_kernel,
        out_shape=pltpu.VMEM((rows, 2 * keys.shape[1]), jnp.bfloat16),
        in_specs=[vmem, vmem],
        out_specs=vmem,
        name="join",
    )(keys, values)
    kv_parts = [kv_own, *swaps_along(kv_own, "kvring")]
    order, far, near, rest, bias = pl.pallas_call(
        functools.partial(prep_kernel, rows, nq, nz),
        out_shape=(
            pltpu.SMEM((heads + 1,), jnp.int32),
            *(slots_in_vmem(slots) for slots in (FAR_SLOTS, NEAR_SLOTS, rest_slots)),
            pltpu.VMEM((quarter, total), jnp.float32),
        ),
        in_specs=[smem, vmem, vmem],
        out_specs=[smem] + [vmem] * 4,
        cost_estimate=cost(4),
        name="prep",
    )(head_mask, doc_ids, queries)
    many = jnp.sum(head_mask) > NEAR_SLOTS + FAR_SLOTS
    *kv_parts, near, order, many = lax.optimization_barrier((*kv_parts, near, order, many))
    kv0 = jnp.concatenate(kv_parts, axis=0)
    kv2 = swap_along(kv0, "qring", 2)
    near_parts = [near, *swaps_along(near, "kvring")]
    rest_all = lax.cond(
        many,
        lambda array: jnp.concatenate([array, *swaps_along(array, "kvring")]),
        lambda array: jnp.zeros((nz * rest_slots, rows, HD), array.dtype),
        lax.optimization_barrier((rest, kv0))[0],
    )
    near_parts[1], kv2, rest_all = lax.optimization_barrier((near_parts[1], kv2, rest_all))
    kv02 = jnp.concatenate([kv0, kv2], axis=0)
    kv = (kv02, swap_along(kv02, "qring", 1))
    far_own = pl.pallas_call(
        functools.partial(own_kernel, len(kv)),
        out_shape=slots_in_vmem(FAR_SLOTS),
        in_specs=[smem] + [vmem] * (len(kv) + 2),
        out_specs=vmem,
        compiler_params=params,
        cost_estimate=cost(2),
        name="own",
    )(order, *in_vmem(*kv, far, bias))
    far_parts = [far_own, *swaps_along(far_own, "kvring")]
    near_slots = heads - FAR_SLOTS
    early_rows = EARLY_PARTS * rows
    late_rows = quarter - early_rows
    order_early = lax.optimization_barrier((order, far_own))[0]
    hbm = pl.BlockSpec(memory_space=pltpu.HBM)
    early, w_near = pl.pallas_call(
        functools.partial(early_kernel, len(kv)),
        out_shape=(
            pltpu.VMEM((near_slots, early_rows, HD), jnp.bfloat16),
            pltpu.VMEM((near_slots * HD, width), jnp.bfloat16),
        ),
        in_specs=[smem] + [vmem] * (len(kv) + EARLY_PARTS + 2) + [hbm],
        out_specs=(vmem, vmem),
        scratch_shapes=[
            pltpu.VMEM((near_slots, early_rows, HD), jnp.bfloat16),
            pltpu.VMEM((PAIR, early_rows, total), jnp.float32),
            pltpu.SemaphoreType.DMA((near_slots,)),
        ],
        compiler_params=params,
        cost_estimate=cost(EARLY_COST),
        name="early",
    )(order_early, *in_vmem(*kv, *near_parts[:EARLY_PARTS], rest_all, bias), pltpu.with_memory_space_constraint(w_out, pltpu.HBM))
    acc, w_far = pl.pallas_call(
        functools.partial(first_kernel, len(kv), nz),
        out_shape=(
            pltpu.VMEM((quarter, width), jnp.float32),
            pltpu.VMEM((FAR_SLOTS * HD, width), jnp.bfloat16),
        ),
        in_specs=[smem] + [vmem] * (len(kv) + nz - EARLY_PARTS + 4) + [hbm],
        out_specs=(vmem, vmem),
        scratch_shapes=[
            pltpu.VMEM((near_slots, late_rows, HD), jnp.bfloat16),
            pltpu.VMEM((quarter, PAIR * HD), jnp.bfloat16),
            pltpu.VMEM((PAIR, late_rows, total), jnp.float32),
            pltpu.SemaphoreType.DMA((FAR_SLOTS,)),
        ],
        compiler_params=params,
        cost_estimate=cost(FIRST_COST),
        name="first",
    )(order, *in_vmem(*kv, *near_parts[EARLY_PARTS:], rest_all, early, bias, w_near), pltpu.with_memory_space_constraint(w_out, pltpu.HBM))
    return pl.pallas_call(
        functools.partial(last_kernel, nz),
        out_shape=jax.ShapeDtypeStruct((quarter, width), jnp.bfloat16),
        in_specs=[vmem] * (nz + 2),
        out_specs=hbm,
        scratch_shapes=[
            pltpu.VMEM((quarter, FAR_SLOTS * HD), jnp.bfloat16),
            pltpu.VMEM((quarter, width), jnp.bfloat16),
            pltpu.SemaphoreType.DMA((width // LAST_TILE,)),
        ],
        compiler_params=params,
        name="last",
    )(*in_vmem(*far_parts[::-1], w_far, acc))


def solution(mesh):
    placed = (
        P(("groups", "qring", "kvring"), "head"),
        P(("groups", "qring", "kvring"), "head"),
        P(("groups", "qring", "kvring"), "head"),
        P("groups"),
        P("head"),
        P("head", "kvring"),
    )
    per_device = per_device_small_ring if small_ring(mesh) else per_device_any_ring
    return jax.shard_map(
        per_device,
        mesh=mesh,
        in_specs=placed,
        out_specs=P(("groups", "qring", "head"), "kvring"),
        check_vma=False,
    )
```

```python
import functools
import math

import jax
import jax.numpy as jnp
from jax import lax
from jax.experimental import pallas as pl
from jax.experimental.pallas import tpu as pltpu
from jax.sharding import PartitionSpec as P

HD = 128


NEG = -1e30


def block_rows(total_rows, shard_rows):
    best_size = shard_rows
    for multiple in range(1, total_rows // shard_rows + 1):
        if total_rows // shard_rows % multiple == 0 and multiple * shard_rows <= 256:
            best_size = multiple * shard_rows
    return best_size


def attend_keys(state, visible, queries4, key_rows, value_rows, scale_factor):
    run_max, run_sum, run_out = state
    mask4 = visible[:, None, None, :]
    scores = (
        jnp.einsum("rgec,kgc->rgek", queries4, key_rows, preferred_element_type=jnp.float32)
        * scale_factor
    )
    scores = jnp.where(mask4, scores, NEG)
    new_max = jnp.maximum(run_max, jnp.max(scores, axis=-1))
    weights = jnp.where(mask4, jnp.exp(scores - new_max[..., None]), 0.0)
    shrink = jnp.exp(run_max - new_max)
    run_sum = run_sum * shrink + jnp.sum(weights, axis=-1)
    update = jnp.einsum(
        "rgek,kgc->rgec",
        weights.astype(jnp.bfloat16),
        value_rows,
        preferred_element_type=jnp.float32,
    )
    run_out = run_out * shrink[..., None] + update
    return (new_max, run_sum, run_out)


def fold_piece(
    state, pieces, key_start, queries4, query_doc, query_pos, doc_ids, shard_rows, scale_factor
):
    key_all, value_all = pieces
    total_rows = key_all.shape[0]
    block_size = block_rows(total_rows, shard_rows)

    def one_block(index, carry):
        offset = index * block_size
        key_rows = lax.dynamic_slice_in_dim(key_all, offset, block_size, 0)
        value_rows = lax.dynamic_slice_in_dim(value_all, offset, block_size, 0)
        first = key_start + offset
        key_doc = lax.dynamic_slice_in_dim(doc_ids, first, block_size, 0)
        key_pos = first + jnp.arange(block_size, dtype=jnp.int32)
        visible = (query_doc[:, None] == key_doc[None, :]) & (
            key_pos[None, :] <= query_pos[:, None]
        )
        return attend_keys(carry, visible, queries4, key_rows, value_rows, scale_factor)

    return lax.fori_loop(0, total_rows // block_size, one_block, state)


def per_device_any_ring(queries, keys, values, doc_ids, head_mask, w_out):
    shard_rows = queries.shape[0]
    kv_local = keys.shape[1] // HD
    q_local = queries.shape[1] // HD
    per_group = q_local // kv_local
    scale_factor = 1.0 / math.sqrt(HD)
    cycle_size = lax.axis_size("kvring")
    cycle_index = lax.axis_index("kvring")
    loop_index = lax.axis_index("qring")
    quarter = cycle_size * shard_rows
    key_rows = keys.reshape(shard_rows, kv_local, HD)
    value_rows = values.reshape(shard_rows, kv_local, HD)
    loop_size = lax.axis_size("qring")
    gathered = lax.all_gather(queries, "qring", axis=0, tiled=True)
    query_total = loop_size * shard_rows
    row_ids = jnp.arange(query_total, dtype=jnp.int32)
    query_pos = row_ids // shard_rows * quarter + cycle_index * shard_rows + row_ids % shard_rows
    queries4 = gathered.reshape(query_total, kv_local, per_group, HD)
    query_doc = jnp.take(doc_ids, query_pos)
    key_base = loop_index * quarter
    initial = (
        jnp.full((query_total, kv_local, per_group), NEG, jnp.float32),
        jnp.zeros((query_total, kv_local, per_group), jnp.float32),
        jnp.zeros((query_total, kv_local, per_group, HD), jnp.float32),
    )
    run_max, run_sum, run_out = fold_piece(
        initial,
        (
            lax.all_gather(key_rows, "kvring", axis=0, tiled=True),
            lax.all_gather(value_rows, "kvring", axis=0, tiled=True),
        ),
        key_base,
        queries4,
        query_doc,
        query_pos,
        doc_ids,
        shard_rows,
        scale_factor,
    )
    top = lax.pmax(run_max, "qring")
    factor = jnp.exp(run_max - top)
    numer, denom = (
        lax.psum_scatter(
            (run_out * factor[..., None]).astype(jnp.bfloat16),
            "qring",
            scatter_dimension=0,
            tiled=True,
        ).astype(jnp.float32),
        lax.psum_scatter(
            (run_sum * factor).astype(jnp.bfloat16), "qring", scatter_dimension=0, tiled=True
        ).astype(jnp.float32),
    )
    mask_f = head_mask.reshape(kv_local, per_group).astype(jnp.float32)
    attended = (
        (numer / denom[..., None] * mask_f[None, :, :, None])
        .astype(jnp.bfloat16)
        .reshape(shard_rows, q_local * HD)
    )
    partial_sum = jnp.dot(
        lax.all_gather(attended, "kvring", axis=0, tiled=True),
        w_out,
        preferred_element_type=jnp.float32,
    )
    return lax.psum_scatter(
        partial_sum.astype(jnp.bfloat16), "head", scatter_dimension=0, tiled=True
    )


VMEM_LIMIT = 24 * 1024 * 1024
LOG2E = math.log2(math.e)
PAIR = 2
NEAR_SLOTS = 16
EARLY_PARTS = 2
EARLY_COST = 4
FIRST_COST = 6
FAR_SLOTS = 10
TILE = 1024
LAST_TILE = 512


def small_ring(mesh):
    return (mesh.shape["qring"], mesh.shape["kvring"], mesh.shape["head"]) == (4, 4, 1)


def swap_along(array, axis_name, partner):
    size = lax.axis_size(axis_name)
    return lax.ppermute(array, axis_name, [(i, i ^ partner) for i in range(size)])


def partner_of(slot, count):
    return (count - slot) % count


def swaps_along(array, axis_name):
    size = lax.axis_size(axis_name)
    return [swap_along(array, axis_name, partner_of(slot, size)) for slot in range(1, size)]


def in_vmem(*arrays):
    return [pltpu.with_memory_space_constraint(array, pltpu.VMEM) for array in arrays]


def slot_of(index, width, count):
    slot = jnp.zeros_like(index)
    for bound in range(1, count):
        slot = slot + (index >= bound * width).astype(jnp.int32)
    return slot


def rows_of(slot):
    return pl.ds(pl.multiple_of(slot * HD, HD), HD)


def join_kernel(k_ref, v_ref, out_ref):
    width = k_ref.shape[1]
    out_ref[:, :width] = k_ref[...]
    out_ref[:, width:] = v_ref[...]


def prep_kernel(rows, nq, nz, mask_ref, doc_ref, q_ref, order_ref, *refs):
    *slot_refs, bias_ref = refs
    heads = mask_ref.shape[0]
    for slot in range(heads):
        order_ref[slot] = 0
    kept = jnp.int32(0)
    for head in range(heads):
        order_ref[kept] = head
        kept = kept + mask_ref[head]
    order_ref[heads] = kept
    slot = 0
    for ref in slot_refs:
        for place in range(ref.shape[0]):
            ref[place] = q_ref[:, rows_of(order_ref[slot])]
            slot += 1
    quarter = rows * nz
    total = quarter * nq
    q_at = lax.axis_index("qring")
    z_at = lax.axis_index("kvring")
    doc = doc_ref[...].reshape(1, total)
    row = lax.broadcasted_iota(jnp.int32, (quarter, 1), 0)
    row_z = slot_of(row, rows, nz)
    row_pos = q_at * quarter + (partner_of(row_z, nz) ^ z_at) * rows + row - row_z * rows
    col = lax.broadcasted_iota(jnp.int32, (1, total), 1)
    col_q = slot_of(col, quarter, nq)
    rest = col - col_q * quarter
    col_z = slot_of(rest, rows, nz)
    col_pos = (((col_q & 1) * 2 + (col_q >> 1)) ^ q_at) * quarter + (partner_of(col_z, nz) ^ z_at) * rows + rest - col_z * rows
    own_doc = jnp.sum(jnp.where(col == row_pos, doc, 0), axis=1, keepdims=True)
    first = jnp.sum((doc < own_doc).astype(jnp.int32), axis=1, keepdims=True)
    bias_ref[...] = jnp.where((col_pos >= first) & (col_pos <= row_pos), 0.0, NEG)


def kv_at(slot, kv_refs, order_ref, is_value):
    heads = order_ref.shape[0] - 1
    kv_heads = kv_refs[0].shape[1] // (2 * HD)
    group = order_ref[slot] // (heads // kv_heads) + is_value * kv_heads
    return jnp.concatenate([ref[:, rows_of(group)] for ref in kv_refs], axis=0)


def scores_of(q, slot, kv_refs, order_ref):
    k = kv_at(slot, kv_refs, order_ref, 0)
    return lax.dot_general(q, k, (((1,), (1,)), ((), ())), preferred_element_type=jnp.float32)


def attended(scores, bias, slot, kv_refs, order_ref):
    scores = scores * (LOG2E / math.sqrt(HD)) + bias
    weights = jnp.exp2(scores - jnp.max(scores, axis=1, keepdims=True))
    v = kv_at(slot, kv_refs, order_ref, 1)
    v_and_ones = jnp.concatenate([v, jnp.ones_like(v)], axis=1)
    sums = jnp.dot(weights.astype(jnp.bfloat16), v_and_ones, preferred_element_type=jnp.float32)
    keep = (slot < order_ref[order_ref.shape[0] - 1]).astype(jnp.float32)
    return (sums[:, :HD] * (keep / sums[:, HD:])).astype(jnp.bfloat16)


def own_kernel(kvs, order_ref, *refs):
    kv_refs, (q_ref, bias_ref, att_ref) = refs[:kvs], refs[kvs:]
    rows = q_ref.shape[1]

    def one_slot(slot):
        scores = scores_of(q_ref[slot], slot, kv_refs, order_ref)
        att_ref[slot] = attended(scores, bias_ref[:rows], slot, kv_refs, order_ref)

    pl.loop(0, FAR_SLOTS, unroll=FAR_SLOTS)(one_slot)


def pairs_of(order_ref):
    heads = order_ref.shape[0] - 1
    rest_slots = heads - FAR_SLOTS - NEAR_SLOTS
    extra = jnp.clip((order_ref[heads] - FAR_SLOTS - NEAR_SLOTS + PAIR - 1) // PAIR, 0, rest_slots // PAIR)
    return NEAR_SLOTS // PAIR + extra, extra


def place_queries(parts, extra, near_refs, rest_ref, q_ref):
    rest_slots = q_ref.shape[0] - NEAR_SLOTS
    for slot in range(NEAR_SLOTS):
        q_ref[slot] = jnp.concatenate([ref[slot] for ref in near_refs], axis=0)

    @pl.when(extra > 0)
    def _():
        for slot in range(rest_slots):
            rows = [rest_ref[part * rest_slots + slot] for part in parts]
            q_ref[NEAR_SLOTS + slot] = jnp.concatenate(rows, axis=0)


def attend_pairs(pairs, q_ref, score_ref, bias, kv_refs, order_ref, keep, between):
    def score(pair, place):
        slot = pair * PAIR + place
        score_ref[place] = scores_of(q_ref[slot], FAR_SLOTS + slot, kv_refs, order_ref)

    for place in range(PAIR):
        score(0, place)

    def one_pair(pair):
        later = jnp.minimum(pair + 1, pairs - 1)
        between(pair)
        for place in range(PAIR):
            slot = pair * PAIR + place
            keep(slot, place, attended(score_ref[place], bias, FAR_SLOTS + slot, kv_refs, order_ref))
            score(later, place)

    pl.loop(0, pairs)(one_pair)


def w_copy(order_ref, w_hbm, w_ref, sem, start, slot):
    return pltpu.make_async_copy(w_hbm.at[rows_of(order_ref[start + slot])], w_ref.at[rows_of(slot)], sem.at[slot])


def early_kernel(kvs, order_ref, *refs):
    kv_refs, near_refs = refs[:kvs], refs[kvs : kvs + EARLY_PARTS]
    rest_ref, bias_ref, w_hbm, early_ref, w_ref, q_ref, score_ref, sem = refs[kvs + EARLY_PARTS :]
    pairs, extra = pairs_of(order_ref)
    copy_of = functools.partial(w_copy, order_ref, w_hbm, w_ref, sem, FAR_SLOTS)
    pl.loop(0, pairs * PAIR)(lambda slot: copy_of(slot).start())
    place_queries(range(EARLY_PARTS), extra, near_refs, rest_ref, q_ref)
    rows = q_ref.shape[1]

    def keep(slot, place, rows_attended):
        early_ref[slot] = rows_attended

    attend_pairs(pairs, q_ref, score_ref, bias_ref[:rows], kv_refs, order_ref, keep, lambda pair: None)
    pl.loop(0, pairs * PAIR)(lambda slot: copy_of(slot).wait())


def first_kernel(kvs, nz, order_ref, *refs):
    late = nz - EARLY_PARTS
    kv_refs, near_refs = refs[:kvs], refs[kvs : kvs + late]
    rest_ref, early_ref, bias_ref, w_ref, w_hbm, acc_ref, w_far_ref, q_ref, att_ref, score_ref, sem = refs[kvs + late :]
    pairs, extra = pairs_of(order_ref)
    copy_of = functools.partial(w_copy, order_ref, w_hbm, w_far_ref, sem, 0)
    pl.loop(0, FAR_SLOTS)(lambda slot: copy_of(slot).start())

    place_queries(range(EARLY_PARTS, nz), extra, near_refs, rest_ref, q_ref)
    done = early_ref.shape[1]

    def project(pair):
        rows = pl.ds(pl.multiple_of(pair * PAIR * HD, HD), PAIR * HD)
        for at in range(0, acc_ref.shape[1], TILE):
            acc_ref[:, at : at + TILE] += jnp.dot(
                att_ref[...], w_ref[rows, at : at + TILE], preferred_element_type=jnp.float32
            )

    def keep(slot, place, rows_attended):
        att_ref[:done, place * HD : (place + 1) * HD] = early_ref[slot]
        att_ref[done:, place * HD : (place + 1) * HD] = rows_attended

    def between(pair):
        project(jnp.maximum(pair - 1, 0))

    acc_ref[...] = jnp.zeros_like(acc_ref)
    att_ref[...] = jnp.zeros_like(att_ref)
    attend_pairs(pairs, q_ref, score_ref, bias_ref[done:], kv_refs, order_ref, keep, between)
    project(pairs - 1)
    pl.loop(0, FAR_SLOTS)(lambda slot: copy_of(slot).wait())


def last_kernel(nz, *refs):
    *refs, out_hbm, att_ref, out_ref, sem = refs
    refs = [*refs, out_ref, att_ref]
    copies = []
    att_refs, (w_ref, acc_ref, out_ref, att_ref) = refs[:nz][::-1], refs[nz:]
    for slot in range(FAR_SLOTS):
        att_ref[:, slot * HD : (slot + 1) * HD] = jnp.concatenate([ref[slot] for ref in att_refs], axis=0)
    rows = att_refs[0].shape[1]
    z_at = lax.axis_index("kvring")
    for index, at in enumerate(range(0, acc_ref.shape[1], LAST_TILE)):
        tile = slice(at, at + LAST_TILE)
        mixed = acc_ref[:, tile] + jnp.dot(att_ref[...], w_ref[:, tile], preferred_element_type=jnp.float32)
        mixed = mixed.astype(jnp.bfloat16)
        for slot in range(nz):
            place = pl.multiple_of((z_at ^ partner_of(slot, nz)) * rows, rows)
            out_ref[pl.ds(place, rows), tile] = mixed[slot * rows : (slot + 1) * rows]
        copies.append(pltpu.make_async_copy(out_ref.at[:, tile], out_hbm.at[:, tile], sem.at[index]))
        copies[-1].start()
    for copy in copies:
        copy.wait()


def per_device_small_ring(queries, keys, values, doc_ids, head_mask, w_out):
    rows = queries.shape[0]
    nq = lax.axis_size("qring")
    nz = lax.axis_size("kvring")
    heads = head_mask.shape[0]
    width = w_out.shape[1]
    quarter = rows * nz
    total = quarter * nq
    rest_slots = heads - FAR_SLOTS - NEAR_SLOTS
    smem = pl.BlockSpec(memory_space=pltpu.SMEM)
    vmem = pl.BlockSpec(memory_space=pltpu.VMEM)
    hbm = pl.BlockSpec(memory_space=pltpu.HBM)
    params = pltpu.CompilerParams(vmem_limit_bytes=VMEM_LIMIT)

    def cost(micros):
        return pl.CostEstimate(flops=int(micros * 1e9), bytes_accessed=0, transcendentals=0)

    def slots_in_vmem(slots):
        return pltpu.VMEM((slots, rows, HD), jnp.bfloat16)

    kv_own = pl.pallas_call(
        join_kernel,
        out_shape=pltpu.VMEM((rows, 2 * keys.shape[1]), jnp.bfloat16),
        in_specs=[vmem, vmem],
        out_specs=vmem,
        name="join",
    )(keys, values)
    kv_parts = [kv_own, *swaps_along(kv_own, "kvring")]
    order, far, near, rest, bias = pl.pallas_call(
        functools.partial(prep_kernel, rows, nq, nz),
        out_shape=(
            pltpu.SMEM((heads + 1,), jnp.int32),
            *(slots_in_vmem(slots) for slots in (FAR_SLOTS, NEAR_SLOTS, rest_slots)),
            pltpu.VMEM((quarter, total), jnp.float32),
        ),
        in_specs=[smem, vmem, vmem],
        out_specs=[smem] + [vmem] * 4,
        cost_estimate=cost(4),
        name="prep",
    )(head_mask, doc_ids, queries)
    many = jnp.sum(head_mask) > NEAR_SLOTS + FAR_SLOTS
    *kv_parts, near, order, many = lax.optimization_barrier((*kv_parts, near, order, many))
    kv0 = jnp.concatenate(kv_parts, axis=0)
    kv2 = swap_along(kv0, "qring", 2)
    near_parts = [near, *swaps_along(near, "kvring")]
    rest_all = lax.cond(
        many,
        lambda array: jnp.concatenate([array, *swaps_along(array, "kvring")]),
        lambda array: jnp.zeros((nz * rest_slots, rows, HD), array.dtype),
        lax.optimization_barrier((rest, kv0))[0],
    )
    near_parts[1], kv2, rest_all = lax.optimization_barrier((near_parts[1], kv2, rest_all))
    kv02 = jnp.concatenate([kv0, kv2], axis=0)
    kv = (kv02, swap_along(kv02, "qring", 1))
    far_own = pl.pallas_call(
        functools.partial(own_kernel, len(kv)),
        out_shape=slots_in_vmem(FAR_SLOTS),
        in_specs=[smem] + [vmem] * (len(kv) + 2),
        out_specs=vmem,
        compiler_params=params,
        cost_estimate=cost(0),
        name="own",
    )(order, *in_vmem(*kv, far, bias))
    far_parts = [far_own, *swaps_along(far_own, "kvring")]
    near_slots = heads - FAR_SLOTS
    early_rows = EARLY_PARTS * rows
    late_rows = quarter - early_rows
    order_early = lax.optimization_barrier((order, far_own))[0]
    hbm = pl.BlockSpec(memory_space=pltpu.HBM)
    early, w_near = pl.pallas_call(
        functools.partial(early_kernel, len(kv)),
        out_shape=(
            pltpu.VMEM((near_slots, early_rows, HD), jnp.bfloat16),
            pltpu.VMEM((near_slots * HD, width), jnp.bfloat16),
        ),
        in_specs=[smem] + [vmem] * (len(kv) + EARLY_PARTS + 2) + [hbm],
        out_specs=(vmem, vmem),
        scratch_shapes=[
            pltpu.VMEM((near_slots, early_rows, HD), jnp.bfloat16),
            pltpu.VMEM((PAIR, early_rows, total), jnp.float32),
            pltpu.SemaphoreType.DMA((near_slots,)),
        ],
        compiler_params=params,
        cost_estimate=cost(EARLY_COST),
        name="early",
    )(order_early, *in_vmem(*kv, *near_parts[:EARLY_PARTS], rest_all, bias), pltpu.with_memory_space_constraint(w_out, pltpu.HBM))
    acc, w_far = pl.pallas_call(
        functools.partial(first_kernel, len(kv), nz),
        out_shape=(
            pltpu.VMEM((quarter, width), jnp.float32),
            pltpu.VMEM((FAR_SLOTS * HD, width), jnp.bfloat16),
        ),
        in_specs=[smem] + [vmem] * (len(kv) + nz - EARLY_PARTS + 4) + [hbm],
        out_specs=(vmem, vmem),
        scratch_shapes=[
            pltpu.VMEM((near_slots, late_rows, HD), jnp.bfloat16),
            pltpu.VMEM((quarter, PAIR * HD), jnp.bfloat16),
            pltpu.VMEM((PAIR, late_rows, total), jnp.float32),
            pltpu.SemaphoreType.DMA((FAR_SLOTS,)),
        ],
        compiler_params=params,
        cost_estimate=cost(FIRST_COST),
        name="first",
    )(order, *in_vmem(*kv, *near_parts[EARLY_PARTS:], rest_all, early, bias, w_near), pltpu.with_memory_space_constraint(w_out, pltpu.HBM))
    return pl.pallas_call(
        functools.partial(last_kernel, nz),
        out_shape=jax.ShapeDtypeStruct((quarter, width), jnp.bfloat16),
        in_specs=[vmem] * (nz + 2),
        out_specs=hbm,
        scratch_shapes=[
            pltpu.VMEM((quarter, FAR_SLOTS * HD), jnp.bfloat16),
            pltpu.VMEM((quarter, width), jnp.bfloat16),
            pltpu.SemaphoreType.DMA((width // LAST_TILE,)),
        ],
        compiler_params=params,
        name="last",
    )(*in_vmem(*far_parts[::-1], w_far, acc))


def solution(mesh):
    placed = (
        P(("groups", "qring", "kvring"), "head"),
        P(("groups", "qring", "kvring"), "head"),
        P(("groups", "qring", "kvring"), "head"),
        P("groups"),
        P("head"),
        P("head", "kvring"),
    )
    per_device = per_device_small_ring if small_ring(mesh) else per_device_any_ring
    return jax.shard_map(
        per_device,
        mesh=mesh,
        in_specs=placed,
        out_specs=P(("groups", "qring", "head"), "kvring"),
        check_vma=False,
    )
```
